256 devices in a mesh: lon: 32 (over z, y), lat: 8 (over x, core).
Axes of the slice: x: 4, y: 4, z: 8, core: 2. Of those that a mesh axis runs over, the one named last changes fastest.
Arguments:
- right_side: float32 [2048, 16384], P('lat', 'lon'), may hold values from -6 to 6
- depth_level: int32 [2048, 16384], P('lat', 'lon'), may hold values from 1 to 50
- ocean_mask: int32 [2048, 16384], P('lat', 'lon'), may hold values 0 or 1
Outputs:
- pressure: float32 [2048, 16384], P('lat', 'lon')
- residual: float32 [2048, 16384], P('lat', 'lon')
The draws below stay inside these ranges and needn't reach their ends.
All inputs are finite; a program needn't handle non-finite values. No bound on the sum of `ocean_mask` on one device may be relied on, other than what follows from the above.
Results may differ from the reference program's by a relative error of at most 0.0003.
Values sent between devices are 32-bit elements; how exact they have to be, the bound alone decides.
No kernel may reach another device: no remote copies, remote signals or barrier semaphores. Data moves between devices by JAX's collectives and lax.ppermute only.
A program may use at most 128 MiB of HBM per device.

```python
import jax
import jax.numpy as jnp

LEVELS = 4
SWEEPS = 2
COARSE_SWEEPS = 9
DEPTH_LEVELS = 50
NLAT = 2048
NLON = 16384


def place_ends(result, key, least, high):
    place = [jax.random.randint(jax.random.fold_in(key, axis), (), 0, length) for axis, length in enumerate(result.shape)]
    main_axis = result.shape.index(max(result.shape))
    next_to = place[:main_axis] + [(place[main_axis] + 1) % result.shape[main_axis]] + place[main_axis + 1:]
    return result.at[tuple(place)].set(least).at[tuple(next_to)].set(high)


def level_of(rng, shape, pieces, least, high):
    def one(dim, blocks):
        draws = jax.random.uniform(jax.random.fold_in(jax.random.fold_in(rng, 6), dim), (blocks,), jnp.float32, least / len(pieces), high / len(pieces))
        return jnp.repeat(jnp.exp(draws), shape[dim] // blocks).reshape((-1,) + (1,) * (len(shape) - dim - 1))

    gain = one(*pieces[0])
    for cut in pieces[1:]:
        gain = gain * one(*cut)
    return gain


def bell_draw(key, dims, deviation, most, pieces=(), kind=jnp.bfloat16):
    entries = deviation * jax.random.normal(key, dims, jnp.float32)
    if pieces:
        entries = entries * level_of(key, dims, pieces, -0.22, 0.18)
    return jnp.clip(entries, -most, most).astype(kind)


def setup_inputs(seed: int = 0) -> dict:
    splits = jax.random.split(jax.random.key(seed), 4)
    return {
        "right_side": bell_draw(splits[0], (NLAT, NLON), 1.0, 6.0, ((0, 8), (1, 32)), jnp.float32),
        "depth_level": place_ends(jax.random.randint(splits[1], (NLAT, NLON), 1, DEPTH_LEVELS + 1), jax.random.fold_in(splits[1], 1), 1, DEPTH_LEVELS).astype(jnp.int32),
        "ocean_mask": place_ends((jax.random.randint(splits[2], (NLAT, NLON), 0, 4) < 3).astype(jnp.int32), jax.random.fold_in(splits[2], 1), 0, 1),
    }


OMEGA = 0.8
SIGMA = 1e-5


def neighbours(field):
    east_side = jnp.roll(field, -1, axis=1)
    west_side = jnp.roll(field, 1, axis=1)
    zero_row = jnp.zeros((1, field.shape[1]), field.dtype)
    north_side = jnp.concatenate([field[1:], zero_row], axis=0)
    south_side = jnp.concatenate([zero_row, field[:-1]], axis=0)
    return east_side, west_side, north_side, south_side


def coefficients(height, scale):
    east_side, west_side, north_side, south_side = neighbours(height)
    coef_east = jnp.minimum(height, east_side) * scale
    coef_west = jnp.minimum(height, west_side) * scale
    coef_north = jnp.minimum(height, north_side) * scale
    coef_south = jnp.minimum(height, south_side) * scale
    faces = coef_east + coef_west + coef_north + coef_south
    diagonal = SIGMA + faces
    return coef_east, coef_west, coef_north, coef_south, diagonal, faces


def keep_active(source, coefs):
    return jnp.where(coefs[5] > 0.0, source, jnp.zeros_like(source))


def operate(field, coefs):
    east_side, west_side, north_side, south_side = neighbours(field)
    return coefs[4] * field - coefs[0] * east_side - coefs[1] * west_side - coefs[2] * north_side - coefs[3] * south_side


def jacobi(field, source, coefs):
    return field + OMEGA * (source - operate(field, coefs)) / coefs[4]


def smooth_zero(source, coefs, count):
    field = OMEGA * source / coefs[4]
    for sweep in range(count - 1):
        field = jacobi(field, source, coefs)
    return field


def restrict(field):
    row_count, col_count = field.shape
    return field.reshape(row_count // 2, 2, col_count // 2, 2).mean(axis=(1, 3))


def prolong(field):
    row_count, col_count = field.shape
    return jnp.broadcast_to(field[:, None, :, None], (row_count, 2, col_count, 2)).reshape(row_count * 2, col_count * 2)


def reference(right_side, depth_level, ocean_mask):
    ocean = ocean_mask.astype(jnp.float32)
    height = ocean * depth_level.astype(jnp.float32) / DEPTH_LEVELS
    source = right_side
    saved = []
    for level in range(LEVELS - 1):
        coefs = coefficients(height, 0.25 ** level)
        source = keep_active(source, coefs)
        iterate = smooth_zero(source, coefs, SWEEPS)
        saved.append((iterate, source, coefs))
        source = restrict(source - operate(iterate, coefs))
        height = restrict(height)
    coefs = coefficients(height, 0.25 ** (LEVELS - 1))
    source = keep_active(source, coefs)
    iterate = smooth_zero(source, coefs, COARSE_SWEEPS)
    for level in reversed(range(LEVELS - 1)):
        previous, source, coefs = saved[level]
        iterate = previous + prolong(iterate)
        for sweep in range(SWEEPS):
            iterate = jacobi(iterate, source, coefs)
    source, coefs = saved[0][1], saved[0][2]
    return iterate, source - operate(iterate, coefs)
```

```python
import jax
import jax.numpy as jnp
import numpy as np
from jax import lax
from jax.experimental import pallas as pl
from jax.experimental.pallas import tpu as pltpu
from jax.sharding import PartitionSpec as P

LEVELS = 4
COARSE_SWEEPS = 9
DEPTH_LEVELS = 50
OMEGA = 0.8
SIGMA = 1e-05

CELL = 2 ** (LEVELS - 1)
LANES = 128
SIDE = 128
PAD = SIDE // CELL
EDGE = 4
FAR = 8
ROWS = 32
COLS = 64
TALL = ROWS + 2 * EDGE
STRIP = EDGE * CELL


def east(x):
    return pltpu.roll(x, x.shape[1] - 1, 1)


def west(x):
    return pltpu.roll(x, 1, 1)


def north(x):
    return pltpu.roll(x, x.shape[0] - 1, 0)


def south(x):
    return pltpu.roll(x, 1, 0)


def each(count, body):
    if count <= 2:
        for q in range(count):
            body(q)
    else:
        lax.fori_loop(0, count, lambda q, carry: (body(q), carry)[1], 0)


def whole(ref, q, r):
    return ref[q, r]


def ends(ref, q, r):
    return jnp.concatenate([ref[q, r, 0:8, :], ref[q, r, TALL - 8 : TALL, :]], axis=0)


def close(v, n):
    for r in range(n):
        v[0, r] = south(v[n, r])
        v[n + 1, r] = north(v[1, r])


def find_faces(n, h, ke, kn):
    for r in range(n):
        h[n, r] = north(h[0, r])

    def body(q):
        for r in range(n):
            here = h[q, r]
            ke[q, r] = jnp.minimum(here, h[q, r + 1] if r + 1 < n else east(h[q, 0]))
            kn[q + 1, r] = jnp.minimum(here, h[q + 1, r])

    each(n, body)
    for r in range(n):
        kn[0, r] = south(kn[n, r])


def weigh(faces, source):
    diagonal = SIGMA + faces
    return diagonal, OMEGA / diagonal, jnp.where(faces > 0.0, source, 0.0)


def find_weights(n, ke, kn, source, d, w, s, v=None):
    def body(q):
        for r in range(n):
            kw = ke[q, r - 1] if r else west(ke[q, n - 1])
            faces = (ke[q, r] + kw) + (kn[q + 1, r] + kn[q, r])
            diagonal, weight, kept = weigh(faces, source[q, r])
            d[q, r], w[q, r], s[q, r] = diagonal, weight, kept
            if v is not None:
                v[q + 1, r] = weight * kept

    each(n, body)
    if v is not None:
        close(v, n)


def start(n, w, s, v, get):
    def body(q):
        for r in range(n):
            v[q + 1, r] = get(w, q, r) * get(s, q, r)

    each(n, body)
    close(v, n)


def pull(n, ke, kn, v, q, get):
    ks = [get(ke, q, r) for r in range(n)]
    cs = [v[q + 1, r] for r in range(n)]
    out = []
    for r in range(n):
        kw = ks[r - 1] if r else west(ks[n - 1])
        ve = cs[r + 1] if r + 1 < n else east(cs[0])
        vw = cs[r - 1] if r else west(cs[n - 1])
        out.append(
            (ks[r] * ve + kw * vw)
            + (get(kn, q + 1, r) * v[q + 2, r] + get(kn, q, r) * v[q, r])
        )
    return cs, out


def sweep(n, ke, kn, w, s, v, out, get=whole, also=None):
    def body(q):
        cs, total = pull(n, ke, kn, v, q, get)
        for r in range(n):
            new = (1.0 - OMEGA) * cs[r] + get(w, q, r) * (get(s, q, r) + total[r])
            out[q + 1, r] = new
            if also is not None:
                also(q, r, new)

    each(n, body)
    close(out, n)


def remains(n, ke, kn, d, s, v, q, get):
    cs, total = pull(n, ke, kn, v, q, get)
    return [(get(s, q, r) - get(d, q, r) * cs[r]) + total[r] for r in range(n)]


def restrict(n, ke, kn, d, s, v, get, put):
    def body(q):
        a = remains(n, ke, kn, d, s, v, 2 * q, get)
        b = remains(n, ke, kn, d, s, v, 2 * q + 1, get)
        for r in range(n // 2):
            put(q, r, 0.25 * ((a[2 * r] + a[2 * r + 1]) + (b[2 * r] + b[2 * r + 1])))

    each(n // 2, body)


def coarsen(n, h, put):
    def body(q):
        for r in range(n // 2):
            a = h[2 * q, 2 * r] + h[2 * q, 2 * r + 1]
            b = h[2 * q + 1, 2 * r] + h[2 * q + 1, 2 * r + 1]
            put(q, r, 0.0625 * (a + b))

    each(n // 2, body)


def merged(inner, strips):
    row = lax.broadcasted_iota(jnp.int32, (8, LANES), 0)
    low = jnp.where(row < 6, strips[0:8], inner[0:8])
    high = jnp.where(row >= 2, strips[8:16], inner[TALL - 8 : TALL])
    return jnp.concatenate([low, inner[8 : TALL - 8], high], axis=0)


def dot_parts(x, matrix):
    high = x.astype(jnp.bfloat16)
    low = (x - high.astype(jnp.float32)).astype(jnp.bfloat16)
    return jnp.dot(high, matrix, preferred_element_type=jnp.float32) + jnp.dot(
        low, matrix, preferred_element_type=jnp.float32
    )


def pack_kernel(f_l, f_r, d_l, d_r, m_l, m_r, first, second):
    def fill(to_next, to_previous):
        to_next[0] = f_r[...]
        to_next[1] = (d_r[...] * m_r[...]).astype(jnp.float32)
        to_previous[0] = f_l[...]
        to_previous[1] = (d_l[...] * m_l[...]).astype(jnp.float32)

    even = lax.rem(lax.axis_index("lon"), 2) == 0

    @pl.when(even)
    def _():
        fill(first, second)

    @pl.when(jnp.logical_not(even))
    def _():
        fill(second, first)


def down_kernel(
    f, depth, mask, first, second, split,
    s0, h0, it0, s1, it1, s2, it2, s3, out_first, out_second,
    nat_s, nat_h, h1, h2, ke0, kn0, d0, w0, k0, v0,
    ke1, kn1, d1, w1, k1, v1, ke2, kn2, d2, w2, k2, v2,
):
    even = lax.rem(lax.axis_index("lon"), 2) == 0
    matrix = split[...]
    nothing = jnp.zeros((CELL, STRIP, LANES), jnp.float32)
    for nat in (nat_s, nat_h):
        nat[:, 0:STRIP, :] = nothing
        nat[:, STRIP + ROWS * CELL : TALL * CELL, :] = nothing

    def keep(nat, x):
        for r in range(CELL):
            nat[r, STRIP : STRIP + ROWS * CELL, :] = x[:, r * LANES : (r + 1) * LANES]

    def sides(i):
        a, b = first[i], second[i]
        return jnp.where(even, b, a), jnp.where(even, a, b)

    before, after = sides(0)
    keep(nat_s, dot_parts(jnp.concatenate([before, f[...], after], axis=1), matrix))
    before, after = sides(1)
    level = (depth[...] * mask[...]).astype(jnp.float32)
    level = jnp.concatenate([before, level, after], axis=1).astype(jnp.bfloat16)
    level = jnp.dot(level, matrix, preferred_element_type=jnp.float32)
    keep(nat_h, level * (1.0 / DEPTH_LEVELS))

    for q in range(CELL):
        rows = pl.ds(q, TALL, stride=CELL)
        for r in range(CELL):
            s0[q, r] = nat_s[r, rows, :]
            h0[q, r] = nat_h[r, rows, :]

    def put(ref):
        def at(q, r, x):
            ref[q, r] = x

        return at

    s_next, h_next, h3 = (s1, s2, None), (h1, h2, None), []
    source3 = []
    for i, (n, h, ke, kn, source, d, w, k, v, it) in enumerate(
        (
            (8, h0, ke0, kn0, s0, d0, w0, k0, v0, it0),
            (4, h1, ke1, kn1, s1, d1, w1, k1, v1, it1),
            (2, h2, ke2, kn2, s2, d2, w2, k2, v2, it2),
        )
    ):
        find_faces(n, h, ke, kn)
        find_weights(n, ke, kn, source, d, w, k, v)
        sweep(n, ke, kn, w, k, v, it)
        if i < 2:
            restrict(n, ke, kn, d, k, it, whole, put(s_next[i]))
            coarsen(n, h, put(h_next[i]))
        else:
            restrict(n, ke, kn, d, k, it, whole, lambda q, r, x: source3.append(x))
            coarsen(n, h, lambda q, r, x: h3.append(x))
    s3[...] = source3[0]

    def send(to, row, blocks):
        to[:, 0:STRIP, :] = nat_s[:, row : row + STRIP, :]
        to[:, STRIP : 2 * STRIP, :] = nat_h[:, row : row + STRIP, :]
        for i in range(CELL):
            to[i, 2 * STRIP : 2 * STRIP + 8, :] = blocks[i] if i < len(blocks) else jnp.zeros((8, LANES), jnp.float32)

    s, h = source3[0], h3[0]

    def fill(to_next, to_previous):
        send(to_next, ROWS * CELL, (s[24:32], s[32:40], h[24:32]))
        send(to_previous, STRIP, (s[8:16], s[0:8], h[8:16]))

    even = lax.rem(lax.axis_index("lat"), 2) == 0

    @pl.when(even)
    def _():
        fill(out_first, out_second)

    @pl.when(jnp.logical_not(even))
    def _():
        fill(out_second, out_first)


def up_kernel(
    s0_in, h0_in, it0_in, s1_in, it1_in, s2_in, it2_in, s3_in, first, second, join,
    pressure, residual,
    far, s0, h0, s1, h1, s2, h2, ke0, kn0, d0, w0, k0, e0, g0, a0, b0,
    ke1, kn1, d1, w1, k1, e1, g1, a1, b1, ke2, kn2, d2, w2, k2, e2, g2, a2, b2, flat, nat,
):
    even = lax.rem(lax.axis_index("lat"), 2) == 0
    tops = slice(TALL - EDGE, TALL)

    def own(q):
        for r in range(CELL):
            s0[q, r] = s0_in[q, r]
            h0[q, r] = h0_in[q, r]

    each(CELL, own)

    def fill(low, high):
        for q in range(CELL):
            for r in range(CELL):
                s0[q, r, 0:EDGE, :] = low[r, pl.ds(q, EDGE, stride=CELL), :]
                s0[q, r, tops, :] = high[r, pl.ds(q, EDGE, stride=CELL), :]
                h0[q, r, 0:EDGE, :] = low[r, pl.ds(STRIP + q, EDGE, stride=CELL), :]
                h0[q, r, tops, :] = high[r, pl.ds(STRIP + q, EDGE, stride=CELL), :]
        for i in range(3):
            far[0, i] = low[i, 2 * STRIP : 2 * STRIP + 8, :]
            far[1, i] = high[i, 2 * STRIP : 2 * STRIP + 8, :]

    @pl.when(even)
    def _():
        fill(second, first)

    @pl.when(jnp.logical_not(even))
    def _():
        fill(first, second)

    levels = (
        (8, h0, ke0, kn0, s0, d0, w0, k0, e0, g0, a0, b0, it0_in),
        (4, h1, ke1, kn1, s1, d1, w1, k1, e1, g1, a1, b1, it1_in),
        (2, h2, ke2, kn2, s2, d2, w2, k2, e2, g2, a2, b2, it2_in),
    )
    h3, source3 = [], []
    for i, (n, h, ke, kn, source, d, w, k, e, g, _, _, _) in enumerate(levels):
        find_faces(n, h, ke, kn)
        find_weights(n, ke, kn, source, d, w, k)
        start(n, w, k, e, ends)
        sweep(n, ke, kn, w, k, e, g, ends)
        if i < 2:
            s_next, s_inner, h_next = ((s1, s1_in, h1), (s2, s2_in, h2))[i]

            def put_s(q, r, x, s_next=s_next, s_inner=s_inner):
                s_next[q, r] = merged(s_inner[q, r], x)

            def put_h(q, r, x, h_next=h_next):
                h_next[q, r] = x

            restrict(n, ke, kn, d, k, g, ends, put_s)
            coarsen(n, h, put_h)
        else:
            restrict(n, ke, kn, d, k, g, ends, lambda q, r, x: source3.append(merged(s3_in[...], x)))
            coarsen(n, h, lambda q, r, x: h3.append(x))

    row = lax.broadcasted_iota(jnp.int32, (8, LANES), 0)
    s, h = source3[0], h3[0]
    s = jnp.concatenate(
        [
            far[0, 0],
            jnp.where(row < 2, far[0, 1], s[0:8]),
            s[8 : TALL - 8],
            jnp.where(row >= 6, far[1, 1], s[TALL - 8 : TALL]),
            far[1, 0],
        ],
        axis=0,
    )
    h = jnp.concatenate([far[0, 2], h, far[1, 2]], axis=0)
    ke, kn = jnp.minimum(h, east(h)), jnp.minimum(h, north(h))
    kw, ks = west(ke), south(kn)
    _, weight, s = weigh((ke + kw) + (kn + ks), s)
    v = weight * s
    for _ in range(COARSE_SWEEPS - 1):
        total = (ke * east(v) + kw * west(v)) + (kn * north(v) + ks * south(v))
        v = (1.0 - OMEGA) * v + weight * (s + total)
    coarse = v[FAR : FAR + TALL]

    above = lambda q, r: coarse
    for n, h, ke, kn, source, d, w, k, e, g, a, b, inner in reversed(levels):

        def correct(q, n=n, g=g, a=a, inner=inner, above=above):
            for r in range(n):
                a[q + 1, r] = merged(inner[q + 1, r], g[q + 1, r]) + above(q, r)

        each(n, correct)
        close(a, n)
        sweep(n, ke, kn, w, k, a, b)
        if n < CELL:
            sweep(n, ke, kn, w, k, b, a)
        above = lambda q, r, a=a: a[lax.div(q, 2) + 1, r // 2]

    n, _, ke, kn, _, d, w, k, _, _, a, b, _ = levels[0]

    def flatten(q, r, x):
        flat[pl.ds(pl.multiple_of(q * TALL, 8), TALL), r * LANES : (r + 1) * LANES] = x

    def finish(out):
        res = dot_parts(flat[...], join[...])
        for c in range(nat.shape[0]):
            lanes = slice(c * LANES, (c + 1) * LANES)
            for q in range(CELL):
                nat[c, pl.ds(q, TALL, stride=CELL), :] = res[q * TALL : (q + 1) * TALL, lanes]
            out[:, lanes] = nat[c, STRIP : STRIP + ROWS * CELL, :]

    sweep(n, ke, kn, w, k, b, a, whole, flatten)
    finish(pressure)

    def last(q):
        for r, x in enumerate(remains(n, ke, kn, d, k, a, q, whole)):
            flatten(q, r, x)

    each(n, last)
    finish(residual)


def swap(x, axis, count, offset, closed):
    pairs = []
    for i in range(offset, count, 2):
        if i + 1 < count or closed:
            j = (i + 1) % count
            pairs += [(i, j), (j, i)]
    return lax.ppermute(x, axis, pairs)


def split_matrix(columns):
    out = np.zeros((columns + 2 * SIDE, CELL * LANES), np.float32)
    c = np.arange(columns + 2 * SIDE)
    out[c, (c % CELL) * LANES + c // CELL] = 1.0
    return jnp.asarray(out, jnp.bfloat16)


def join_matrix(columns):
    out = np.zeros((CELL * LANES, columns), np.float32)
    c = np.arange(columns)
    out[(c % CELL) * LANES + c // CELL + PAD, c] = 1.0
    return jnp.asarray(out, jnp.bfloat16)


VMEM = pl.BlockSpec(memory_space=pltpu.VMEM)


def shaped(*dims):
    return jax.ShapeDtypeStruct(dims, jnp.float32)


def planes(n, more=0, rows=TALL):
    return (n + more, n, rows, LANES)


def buffers(*shapes):
    return [pltpu.VMEM(s, jnp.float32) for s in shapes]


LIMIT = pltpu.CompilerParams(vmem_limit_bytes=48 * 1024 * 1024)


def local(right_side, depth_level, ocean_mask):
    rows, columns = right_side.shape
    lon, lat = lax.axis_size("lon"), lax.axis_size("lat")
    left = pl.BlockSpec((rows, SIDE), lambda i: (0, 0))
    right = pl.BlockSpec((rows, SIDE), lambda i: (0, columns // SIDE - 1))
    first, second = pl.pallas_call(
        pack_kernel,
        grid=(1,),
        out_shape=[shaped(2, rows, SIDE)] * 2,
        in_specs=[left, right] * 3,
        out_specs=[VMEM] * 2,
    )(right_side, right_side, depth_level, depth_level, ocean_mask, ocean_mask)
    first = swap(first, "lon", lon, 0, True)
    second = swap(second, "lon", lon, 1, True)

    wide = CELL * LANES
    message = shaped(CELL, 2 * STRIP + 8, LANES)
    outs = pl.pallas_call(
        down_kernel,
        out_shape=[
            shaped(*planes(8)), shaped(*planes(8, 1)), shaped(*planes(8, 2)),
            shaped(*planes(4)), shaped(*planes(4, 2)),
            shaped(*planes(2)), shaped(*planes(2, 2)),
            shaped(TALL, LANES), message, message,
        ],
        in_specs=[VMEM] * 6,
        out_specs=[VMEM] * 10,
        scratch_shapes=buffers(
            (CELL, TALL * CELL, LANES), (CELL, TALL * CELL, LANES), planes(4, 1), planes(2, 1),
            *[s for n in (8, 4, 2) for s in (planes(n), planes(n, 1), planes(n), planes(n), planes(n), planes(n, 2))],
        ),
        compiler_params=LIMIT,
    )(right_side, depth_level, ocean_mask, first, second, split_matrix(columns))
    *fields, first, second = outs
    first = swap(first, "lat", lat, 0, False)
    second = swap(second, "lat", lat, 1, False)
    return pl.pallas_call(
        up_kernel,
        out_shape=[shaped(rows, columns)] * 2,
        in_specs=[VMEM] * 11,
        out_specs=[VMEM] * 2,
        scratch_shapes=buffers(
            (2, 3, 8, LANES),
            *[s for n in (8, 4, 2) for s in (planes(n), planes(n, 1))],
            *[
                s
                for n in (8, 4, 2)
                for s in (
                    planes(n), planes(n, 1), planes(n), planes(n), planes(n),
                    planes(n, 2, 16), planes(n, 2, 16), planes(n, 2), planes(n, 2),
                )
            ],
            (TALL * CELL, wide), (columns // LANES, TALL * CELL, LANES),
        ),
        compiler_params=LIMIT,
    )(*fields, first, second, join_matrix(columns))


def solution(mesh):
    placed = (P("lat", "lon"), P("lat", "lon"), P("lat", "lon"))
    return jax.shard_map(
        local,
        mesh=mesh,
        in_specs=placed,
        out_specs=(P("lat", "lon"), P("lat", "lon")),
        check_vma=False,
    )
```

```python
import jax
import jax.numpy as jnp
import numpy as np
from jax import lax
from jax.experimental import pallas as pl
from jax.experimental.pallas import tpu as pltpu
from jax.sharding import PartitionSpec as P

LEVELS = 4
COARSE_SWEEPS = 9
DEPTH_LEVELS = 50
OMEGA = 0.8
SIGMA = 1e-05

CELL = 2 ** (LEVELS - 1)
LANES = 128
SIDE = 128
PAD = SIDE // CELL
EDGE = 4
FAR = 8
ROWS = 32
COLS = 64
TALL = ROWS + 2 * EDGE
STRIP = EDGE * CELL


def east(x):
    return pltpu.roll(x, x.shape[1] - 1, 1)


def west(x):
    return pltpu.roll(x, 1, 1)


def north(x):
    return pltpu.roll(x, x.shape[0] - 1, 0)


def south(x):
    return pltpu.roll(x, 1, 0)


def each(count, body):
    for q in range(count):
        body(q)


def whole(ref, q, r):
    return ref[q, r]


def ends(ref, q, r):
    return jnp.concatenate([ref[q, r, 0:8, :], ref[q, r, TALL - 8 : TALL, :]], axis=0)


def close(v, n):
    for r in range(n):
        v[0, r] = south(v[n, r])
        v[n + 1, r] = north(v[1, r])


def find_faces(n, h, ke, kn):
    for r in range(n):
        h[n, r] = north(h[0, r])

    def body(q):
        for r in range(n):
            here = h[q, r]
            ke[q, r] = jnp.minimum(here, h[q, r + 1] if r + 1 < n else east(h[q, 0]))
            kn[q + 1, r] = jnp.minimum(here, h[q + 1, r])

    each(n, body)
    for r in range(n):
        kn[0, r] = south(kn[n, r])


def weigh(faces, source):
    diagonal = SIGMA + faces
    return diagonal, OMEGA / diagonal, jnp.where(faces > 0.0, source, 0.0)


def find_weights(n, ke, kn, source, d, w, s, v=None):
    def body(q):
        for r in range(n):
            kw = ke[q, r - 1] if r else west(ke[q, n - 1])
            faces = (ke[q, r] + kw) + (kn[q + 1, r] + kn[q, r])
            diagonal, weight, kept = weigh(faces, source[q, r])
            d[q, r], w[q, r], s[q, r] = diagonal, weight, kept
            if v is not None:
                v[q + 1, r] = weight * kept

    each(n, body)
    if v is not None:
        close(v, n)


def start(n, w, s, v, get):
    def body(q):
        for r in range(n):
            v[q + 1, r] = get(w, q, r) * get(s, q, r)

    each(n, body)
    close(v, n)


def pull(n, ke, kn, v, q, get):
    ks = [get(ke, q, r) for r in range(n)]
    cs = [v[q + 1, r] for r in range(n)]
    out = []
    for r in range(n):
        kw = ks[r - 1] if r else west(ks[n - 1])
        ve = cs[r + 1] if r + 1 < n else east(cs[0])
        vw = cs[r - 1] if r else west(cs[n - 1])
        out.append(
            (ks[r] * ve + kw * vw)
            + (get(kn, q + 1, r) * v[q + 2, r] + get(kn, q, r) * v[q, r])
        )
    return cs, out


def sweep(n, ke, kn, w, s, v, out, get=whole, also=None):
    def body(q):
        cs, total = pull(n, ke, kn, v, q, get)
        for r in range(n):
            new = (1.0 - OMEGA) * cs[r] + get(w, q, r) * (get(s, q, r) + total[r])
            out[q + 1, r] = new
            if also is not None:
                also(q, r, new)

    each(n, body)
    close(out, n)


def remains(n, ke, kn, d, s, v, q, get):
    cs, total = pull(n, ke, kn, v, q, get)
    return [(get(s, q, r) - get(d, q, r) * cs[r]) + total[r] for r in range(n)]


def restrict(n, ke, kn, d, s, v, get, put):
    def body(q):
        a = remains(n, ke, kn, d, s, v, 2 * q, get)
        b = remains(n, ke, kn, d, s, v, 2 * q + 1, get)
        for r in range(n // 2):
            put(q, r, 0.25 * ((a[2 * r] + a[2 * r + 1]) + (b[2 * r] + b[2 * r + 1])))

    each(n // 2, body)


def coarsen(n, h, put):
    def body(q):
        for r in range(n // 2):
            a = h[2 * q, 2 * r] + h[2 * q, 2 * r + 1]
            b = h[2 * q + 1, 2 * r] + h[2 * q + 1, 2 * r + 1]
            put(q, r, 0.0625 * (a + b))

    each(n // 2, body)


def merged(inner, strips):
    row = lax.broadcasted_iota(jnp.int32, (8, LANES), 0)
    low = jnp.where(row < 6, strips[0:8], inner[0:8])
    high = jnp.where(row >= 2, strips[8:16], inner[TALL - 8 : TALL])
    return jnp.concatenate([low, inner[8 : TALL - 8], high], axis=0)


def dot_parts(x, matrix):
    high = x.astype(jnp.bfloat16)
    low = (x - high.astype(jnp.float32)).astype(jnp.bfloat16)
    return jnp.dot(high, matrix, preferred_element_type=jnp.float32) + jnp.dot(
        low, matrix, preferred_element_type=jnp.float32
    )


def pack_kernel(f_l, f_r, d_l, d_r, m_l, m_r, first, second):
    def fill(to_next, to_previous):
        to_next[0] = f_r[...]
        to_next[1] = (d_r[...] * m_r[...]).astype(jnp.float32)
        to_previous[0] = f_l[...]
        to_previous[1] = (d_l[...] * m_l[...]).astype(jnp.float32)

    even = lax.rem(lax.axis_index("lon"), 2) == 0

    @pl.when(even)
    def _():
        fill(first, second)

    @pl.when(jnp.logical_not(even))
    def _():
        fill(second, first)


def down_kernel(
    f, depth, mask, first, second, split,
    s0, h0, it0, s1, it1, s2, it2, s3, out_first, out_second,
    nat_s, nat_h, h1, h2, ke0, kn0, d0, w0, k0, v0,
    ke1, kn1, d1, w1, k1, v1, ke2, kn2, d2, w2, k2, v2,
):
    even = lax.rem(lax.axis_index("lon"), 2) == 0
    matrix = split[...]
    nothing = jnp.zeros((CELL, STRIP, LANES), jnp.float32)
    for nat in (nat_s, nat_h):
        nat[:, 0:STRIP, :] = nothing
        nat[:, STRIP + ROWS * CELL : TALL * CELL, :] = nothing

    def keep(nat, x):
        for r in range(CELL):
            nat[r, STRIP : STRIP + ROWS * CELL, :] = x[:, r * LANES : (r + 1) * LANES]

    def sides(i):
        a, b = first[i], second[i]
        return jnp.where(even, b, a), jnp.where(even, a, b)

    before, after = sides(0)
    keep(nat_s, dot_parts(jnp.concatenate([before, f[...], after], axis=1), matrix))
    before, after = sides(1)
    level = (depth[...] * mask[...]).astype(jnp.float32)
    level = jnp.concatenate([before, level, after], axis=1).astype(jnp.bfloat16)
    level = jnp.dot(level, matrix, preferred_element_type=jnp.float32)
    keep(nat_h, level * (1.0 / DEPTH_LEVELS))

    for q in range(CELL):
        rows = pl.ds(q, TALL, stride=CELL)
        for r in range(CELL):
            s0[q, r] = nat_s[r, rows, :]
            h0[q, r] = nat_h[r, rows, :]

    def put(ref):
        def at(q, r, x):
            ref[q, r] = x

        return at

    s_next, h_next, h3 = (s1, s2, None), (h1, h2, None), []
    source3 = []
    for i, (n, h, ke, kn, source, d, w, k, v, it) in enumerate(
        (
            (8, h0, ke0, kn0, s0, d0, w0, k0, v0, it0),
            (4, h1, ke1, kn1, s1, d1, w1, k1, v1, it1),
            (2, h2, ke2, kn2, s2, d2, w2, k2, v2, it2),
        )
    ):
        find_faces(n, h, ke, kn)
        find_weights(n, ke, kn, source, d, w, k, v)
        sweep(n, ke, kn, w, k, v, it)
        if i < 2:
            restrict(n, ke, kn, d, k, it, whole, put(s_next[i]))
            coarsen(n, h, put(h_next[i]))
        else:
            restrict(n, ke, kn, d, k, it, whole, lambda q, r, x: source3.append(x))
            coarsen(n, h, lambda q, r, x: h3.append(x))
    s3[...] = source3[0]

    def send(to, row, blocks):
        to[:, 0:STRIP, :] = nat_s[:, row : row + STRIP, :]
        to[:, STRIP : 2 * STRIP, :] = nat_h[:, row : row + STRIP, :]
        for i in range(CELL):
            to[i, 2 * STRIP : 2 * STRIP + 8, :] = blocks[i] if i < len(blocks) else jnp.zeros((8, LANES), jnp.float32)

    s, h = source3[0], h3[0]

    def fill(to_next, to_previous):
        send(to_next, ROWS * CELL, (s[24:32], s[32:40], h[24:32]))
        send(to_previous, STRIP, (s[8:16], s[0:8], h[8:16]))

    even = lax.rem(lax.axis_index("lat"), 2) == 0

    @pl.when(even)
    def _():
        fill(out_first, out_second)

    @pl.when(jnp.logical_not(even))
    def _():
        fill(out_second, out_first)


def up_kernel(
    s0_in, h0_in, it0_in, s1_in, it1_in, s2_in, it2_in, s3_in, first, second, join,
    pressure, residual,
    far, s0, h0, s1, h1, s2, h2, ke0, kn0, d0, w0, k0, e0, g0, a0, b0,
    ke1, kn1, d1, w1, k1, e1, g1, a1, b1, ke2, kn2, d2, w2, k2, e2, g2, a2, b2, flat, nat,
):
    even = lax.rem(lax.axis_index("lat"), 2) == 0
    tops = slice(TALL - EDGE, TALL)

    def own(q):
        for r in range(CELL):
            s0[q, r] = s0_in[q, r]
            h0[q, r] = h0_in[q, r]

    each(CELL, own)

    def fill(low, high):
        for q in range(CELL):
            for r in range(CELL):
                s0[q, r, 0:EDGE, :] = low[r, pl.ds(q, EDGE, stride=CELL), :]
                s0[q, r, tops, :] = high[r, pl.ds(q, EDGE, stride=CELL), :]
                h0[q, r, 0:EDGE, :] = low[r, pl.ds(STRIP + q, EDGE, stride=CELL), :]
                h0[q, r, tops, :] = high[r, pl.ds(STRIP + q, EDGE, stride=CELL), :]
        for i in range(3):
            far[0, i] = low[i, 2 * STRIP : 2 * STRIP + 8, :]
            far[1, i] = high[i, 2 * STRIP : 2 * STRIP + 8, :]

    @pl.when(even)
    def _():
        fill(second, first)

    @pl.when(jnp.logical_not(even))
    def _():
        fill(first, second)

    levels = (
        (8, h0, ke0, kn0, s0, d0, w0, k0, e0, g0, a0, b0, it0_in),
        (4, h1, ke1, kn1, s1, d1, w1, k1, e1, g1, a1, b1, it1_in),
        (2, h2, ke2, kn2, s2, d2, w2, k2, e2, g2, a2, b2, it2_in),
    )
    h3, source3 = [], []
    for i, (n, h, ke, kn, source, d, w, k, e, g, _, _, _) in enumerate(levels):
        find_faces(n, h, ke, kn)
        find_weights(n, ke, kn, source, d, w, k)
        start(n, w, k, e, ends)
        sweep(n, ke, kn, w, k, e, g, ends)
        if i < 2:
            s_next, s_inner, h_next = ((s1, s1_in, h1), (s2, s2_in, h2))[i]

            def put_s(q, r, x, s_next=s_next, s_inner=s_inner):
                s_next[q, r] = merged(s_inner[q, r], x)

            def put_h(q, r, x, h_next=h_next):
                h_next[q, r] = x

            restrict(n, ke, kn, d, k, g, ends, put_s)
            coarsen(n, h, put_h)
        else:
            restrict(n, ke, kn, d, k, g, ends, lambda q, r, x: source3.append(merged(s3_in[...], x)))
            coarsen(n, h, lambda q, r, x: h3.append(x))

    row = lax.broadcasted_iota(jnp.int32, (8, LANES), 0)
    s, h = source3[0], h3[0]
    s = jnp.concatenate(
        [
            far[0, 0],
            jnp.where(row < 2, far[0, 1], s[0:8]),
            s[8 : TALL - 8],
            jnp.where(row >= 6, far[1, 1], s[TALL - 8 : TALL]),
            far[1, 0],
        ],
        axis=0,
    )
    h = jnp.concatenate([far[0, 2], h, far[1, 2]], axis=0)
    ke, kn = jnp.minimum(h, east(h)), jnp.minimum(h, north(h))
    kw, ks = west(ke), south(kn)
    _, weight, s = weigh((ke + kw) + (kn + ks), s)
    v = weight * s
    for _ in range(COARSE_SWEEPS - 1):
        total = (ke * east(v) + kw * west(v)) + (kn * north(v) + ks * south(v))
        v = (1.0 - OMEGA) * v + weight * (s + total)
    coarse = v[FAR : FAR + TALL]

    above = lambda q, r: coarse
    for n, h, ke, kn, source, d, w, k, e, g, a, b, inner in reversed(levels):

        def correct(q, n=n, g=g, a=a, inner=inner, above=above):
            for r in range(n):
                a[q + 1, r] = merged(inner[q + 1, r], g[q + 1, r]) + above(q, r)

        each(n, correct)
        close(a, n)
        sweep(n, ke, kn, w, k, a, b)
        if n < CELL:
            sweep(n, ke, kn, w, k, b, a)
        above = lambda q, r, a=a: a[q // 2 + 1, r // 2]

    n, _, ke, kn, _, d, w, k, _, _, a, b, _ = levels[0]

    def flatten(q, r, x):
        flat[q * TALL : (q + 1) * TALL, r * LANES : (r + 1) * LANES] = x

    def finish(out):
        res = dot_parts(flat[...], join[...])
        for c in range(nat.shape[0]):
            lanes = slice(c * LANES, (c + 1) * LANES)
            for q in range(CELL):
                nat[c, pl.ds(q, TALL, stride=CELL), :] = res[q * TALL : (q + 1) * TALL, lanes]
            out[:, lanes] = nat[c, STRIP : STRIP + ROWS * CELL, :]

    sweep(n, ke, kn, w, k, b, a, whole, flatten)
    finish(pressure)

    def last(q):
        for r, x in enumerate(remains(n, ke, kn, d, k, a, q, whole)):
            flatten(q, r, x)

    each(n, last)
    finish(residual)


def swap(x, axis, count, offset, closed):
    pairs = []
    for i in range(offset, count, 2):
        if i + 1 < count or closed:
            j = (i + 1) % count
            pairs += [(i, j), (j, i)]
    return lax.ppermute(x, axis, pairs)


def split_matrix(columns):
    out = np.zeros((columns + 2 * SIDE, CELL * LANES), np.float32)
    c = np.arange(columns + 2 * SIDE)
    out[c, (c % CELL) * LANES + c // CELL] = 1.0
    return jnp.asarray(out, jnp.bfloat16)


def join_matrix(columns):
    out = np.zeros((CELL * LANES, columns), np.float32)
    c = np.arange(columns)
    out[(c % CELL) * LANES + c // CELL + PAD, c] = 1.0
    return jnp.asarray(out, jnp.bfloat16)


VMEM = pl.BlockSpec(memory_space=pltpu.VMEM)


def shaped(*dims):
    return jax.ShapeDtypeStruct(dims, jnp.float32)


def planes(n, more=0, rows=TALL):
    return (n + more, n, rows, LANES)


def buffers(*shapes):
    return [pltpu.VMEM(s, jnp.float32) for s in shapes]


def limit(mib):
    return pltpu.CompilerParams(vmem_limit_bytes=mib * 1024 * 1024)


def local(right_side, depth_level, ocean_mask):
    rows, columns = right_side.shape
    lon, lat = lax.axis_size("lon"), lax.axis_size("lat")
    left = pl.BlockSpec((rows, SIDE), lambda i: (0, 0))
    right = pl.BlockSpec((rows, SIDE), lambda i: (0, columns // SIDE - 1))
    first, second = pl.pallas_call(
        pack_kernel,
        grid=(1,),
        out_shape=[shaped(2, rows, SIDE)] * 2,
        in_specs=[left, right] * 3,
        out_specs=[VMEM] * 2,
        compiler_params=limit(8),
    )(right_side, right_side, depth_level, depth_level, ocean_mask, ocean_mask)
    second = swap(second, "lon", lon, 1, True)
    first = swap(first, "lon", lon, 0, True)

    wide = CELL * LANES
    message = shaped(CELL, 2 * STRIP + 8, LANES)
    outs = pl.pallas_call(
        down_kernel,
        out_shape=[
            shaped(*planes(8)), shaped(*planes(8, 1)), shaped(*planes(8, 2)),
            shaped(*planes(4)), shaped(*planes(4, 2)),
            shaped(*planes(2)), shaped(*planes(2, 2)),
            shaped(TALL, LANES), message, message,
        ],
        in_specs=[VMEM] * 6,
        out_specs=[VMEM] * 10,
        scratch_shapes=buffers(
            (CELL, TALL * CELL, LANES), (CELL, TALL * CELL, LANES), planes(4, 1), planes(2, 1),
            *[s for n in (8, 4, 2) for s in (planes(n), planes(n, 1), planes(n), planes(n), planes(n), planes(n, 2))],
        ),
        compiler_params=limit(30),
    )(right_side, depth_level, ocean_mask, first, second, split_matrix(columns))
    *fields, first, second = outs
    second = swap(second, "lat", lat, 1, False)
    first = swap(first, "lat", lat, 0, False)
    return pl.pallas_call(
        up_kernel,
        out_shape=[shaped(rows, columns)] * 2,
        in_specs=[VMEM] * 11,
        out_specs=[VMEM] * 2,
        scratch_shapes=buffers(
            (2, 3, 8, LANES),
            *[s for n in (8, 4, 2) for s in (planes(n), planes(n, 1))],
            *[
                s
                for n in (8, 4, 2)
                for s in (
                    planes(n), planes(n, 1), planes(n), planes(n), planes(n),
                    planes(n, 2, 16), planes(n, 2, 16), planes(n, 2), planes(n, 2),
                )
            ],
            (TALL * CELL, wide), (columns // LANES, TALL * CELL, LANES),
        ),
        compiler_params=limit(30),
    )(*fields, first, second, join_matrix(columns))


def solution(mesh):
    placed = (P("lat", "lon"), P("lat", "lon"), P("lat", "lon"))
    return jax.shard_map(
        local,
        mesh=mesh,
        in_specs=placed,
        out_specs=(P("lat", "lon"), P("lat", "lon")),
        check_vma=False,
    )
```

```python
import jax
import jax.numpy as jnp
import numpy as np
from jax import lax
from jax.experimental import pallas as pl
from jax.experimental.pallas import tpu as pltpu
from jax.sharding import PartitionSpec as P

LEVELS = 4
COARSE_SWEEPS = 9
DEPTH_LEVELS = 50
OMEGA = 0.8
SIGMA = 1e-05

CELL = 2 ** (LEVELS - 1)
LANES = 128
SIDE = 96
LEAD = 16
ROWS = 32
COLS = 64
TALL = ROWS + 8


def east(x):
    return pltpu.roll(x, x.shape[1] - 1, 1)


def west(x):
    return pltpu.roll(x, 1, 1)


def north(x):
    return pltpu.roll(x, x.shape[0] - 1, 0)


def south(x):
    return pltpu.roll(x, 1, 0)


def row_of(x):
    return lax.broadcasted_iota(jnp.int32, x.shape, 0)


def lane_of(x):
    return lax.broadcasted_iota(jnp.int32, x.shape, 1)


class Whole:
    def __init__(self, inner, strip, count=TALL):
        self.inner, self.strip, self.count = inner, strip, count

    def __getitem__(self, at):
        q, r = at
        parts = [self.strip[q, r, 16:24, :], self.inner[q, r, 8:24, :], self.strip[q, r, 0 : self.count - 24, :]]
        return jnp.concatenate(parts, axis=0)


def strip_of(x):
    return jnp.concatenate([x[24:TALL], x[0:8]], axis=0)


def merged(inner, strip):
    low = jnp.where(row_of(strip[0:8]) < 2, strip[16:24], inner[0:8])
    high = jnp.where(row_of(strip[0:8]) >= 6, strip[0:8], inner[24:32])
    return jnp.concatenate([low, inner[8:24], high, strip[8:16]], axis=0)


def close(v, n):
    for r in range(n):
        v[0, r] = south(v[n, r])
        v[n + 1, r] = north(v[1, r])


def find_faces(n, h, ke, kn):
    for q in range(n):
        for r in range(n):
            here = h[q, r]
            ke[q, r] = jnp.minimum(here, h[q, r + 1] if r + 1 < n else east(h[q, 0]))
            kn[q + 1, r] = jnp.minimum(here, h[q + 1, r])


def weigh(faces, source):
    diagonal = SIGMA + faces
    return diagonal, OMEGA / diagonal, jnp.where(faces > 0.0, source, 0.0)


def find_weights(n, ke, kn, source, d, w, s, v):
    for q in range(n):
        for r in range(n):
            kw = ke[q, r - 1] if r else west(ke[q, n - 1])
            faces = (ke[q, r] + kw) + (kn[q + 1, r] + kn[q, r])
            diagonal, weight, kept = weigh(faces, source[q, r])
            d[q, r], w[q, r], s[q, r] = diagonal, weight, kept
            v[q + 1, r] = weight * kept
    close(v, n)


def pull(n, ke, kn, v, q, count=None):
    ks = [ke[q, r] for r in range(n)]
    cs = [v[q + 1, r][:count] for r in range(n)]
    out = []
    for r in range(n):
        kw = ks[r - 1] if r else west(ks[n - 1])
        ve = cs[r + 1] if r + 1 < n else east(cs[0])
        vw = cs[r - 1] if r else west(cs[n - 1])
        out.append((ks[r] * ve + kw * vw) + (kn[q + 1, r] * v[q + 2, r][:count] + kn[q, r] * v[q, r][:count]))
    return cs, out


def sweep(n, ke, kn, w, s, v, out, also=None):
    for q in range(n):
        cs, total = pull(n, ke, kn, v, q)
        for r in range(n):
            new = (1.0 - OMEGA) * cs[r] + w[q, r] * (s[q, r] + total[r])
            out[q + 1, r] = new
        if also is not None:
            also(q, [out[q + 1, r][:ROWS] for r in range(n)])
    close(out, n)


def remains(n, ke, kn, d, s, v, q, count=None):
    cs, total = pull(n, ke, kn, v, q, count)
    return [(s[q, r] - d[q, r] * cs[r]) + total[r] for r in range(n)]


def restrict(n, ke, kn, d, s, v, put):
    for q in range(n // 2):
        a = remains(n, ke, kn, d, s, v, 2 * q)
        b = remains(n, ke, kn, d, s, v, 2 * q + 1)
        for r in range(n // 2):
            put(q, r, 0.25 * ((a[2 * r] + a[2 * r + 1]) + (b[2 * r] + b[2 * r + 1])))


def coarsen(n, h, put):
    for q in range(n // 2):
        for r in range(n // 2):
            a = h[2 * q, 2 * r] + h[2 * q, 2 * r + 1]
            b = h[2 * q + 1, 2 * r] + h[2 * q + 1, 2 * r + 1]
            put(q, r, 0.0625 * (a + b))


def dot_parts(x, matrix, parts):
    out = 0.0
    for part in range(parts):
        piece = x.astype(jnp.bfloat16)
        out = out + jnp.dot(piece, matrix, preferred_element_type=jnp.float32)
        if part + 1 < parts:
            x = x - piece.astype(jnp.float32)
    return out


def fold(blocks, free):
    return [jnp.where(free, pltpu.roll(blocks[3], 96 - 32 * i, 1), blocks[i]) for i in range(3)]


def unfold(three, first):
    lane = lane_of(three[0])
    a, b, c = (pltpu.roll(x, 32 * (i + 1), 1) for i, x in enumerate(three))
    return list(three) + [jnp.where(lane < first + 32, a, jnp.where(lane < first + 64, b, c))]


def by_parity(axis, fill, first, second):
    even = lax.rem(lax.axis_index(axis), 2) == 0

    @pl.when(even)
    def _():
        fill(first, second)

    @pl.when(jnp.logical_not(even))
    def _():
        fill(second, first)


def pack_kernel(f, depth, mask, first, second, fs, ds, ms, sems):
    last = f.shape[1] - LANES
    copies = []
    for j, column in enumerate((0, last)):
        for i, (source, to) in enumerate(((f, fs), (depth, ds), (mask, ms))):
            copies.append(pltpu.make_async_copy(source.at[:, column : column + LANES], to.at[j], sems.at[j, i]))
    for copy in copies:
        copy.start()
    for copy in copies:
        copy.wait()

    def fill(to_next, to_previous):
        for j, to in enumerate((to_previous, to_next)):
            count = ROWS * CELL // 4
            s_blocks, h_blocks = [], []
            for block in range(4):
                s_rows, h_rows = [], []
                for q in (2 * block, 2 * block + 1):
                    rows = pl.ds(q, ROWS, stride=CELL)
                    s_rows.append(fs[j, rows, :])
                    h_rows.append((ds[j, rows, :] * ms[j, rows, :]).astype(jnp.float32))
                s_blocks.append(jnp.concatenate(s_rows, axis=0))
                h_blocks.append(jnp.concatenate(h_rows, axis=0))
            lane = lane_of(s_blocks[0])
            free = lane < LANES - SIDE if j else lane >= SIDE
            for k, blocks in enumerate((s_blocks, h_blocks)):
                for i, x in enumerate(fold(blocks, free)):
                    to[k, i * count : (i + 1) * count, :] = x

    by_parity("lon", fill, first, second)


def own_kernel(f, depth, mask, split, s0, h0, nat_s, nat_h):
    matrix = split[...]
    tiles = nat_s.shape[0]
    for c in range(tiles):
        lanes = slice(c * LANES, (c + 1) * LANES)
        nat_s[c] = f[:, lanes]
        nat_h[c] = (depth[:, lanes] * mask[:, lanes]).astype(jnp.float32)
    for nat, out, parts in ((nat_s, s0, 3), (nat_h, h0, 1)):
        rows = [
            jnp.concatenate([nat[c, pl.ds(q, ROWS, stride=CELL), :] for c in range(tiles)], axis=1) for q in range(CELL)
        ]
        x = dot_parts(jnp.concatenate(rows, axis=0), matrix, parts)
        for q in range(CELL):
            for r in range(CELL):
                out[q, r] = x[q * ROWS : (q + 1) * ROWS, r * LANES : (r + 1) * LANES]


def down_kernel(
    first, second, s_own, h_own, split,
    s0, h0, s1, h1, s2, h2, s3, it0, it1, it2,
    ke0, kn0, d0, w0, k0, ke1, kn1, d1, w1, k1, ke2, kn2, d2, w2, k2, out_first, out_second,
    v0, v1, v2,
):
    even = lax.rem(lax.axis_index("lon"), 2) == 0
    matrix = split[...]
    count = ROWS * CELL // 4

    def sides(k):
        before, after = [], []
        for i in range(3):
            rows = slice(i * count, (i + 1) * count)
            a, b = first[k, rows, :], second[k, rows, :]
            before.append(jnp.where(even, b, a))
            after.append(jnp.where(even, a, b))
        before = jnp.concatenate(unfold(before, LANES - SIDE), axis=0)
        after = jnp.concatenate(unfold(after, 0), axis=0)
        return jnp.concatenate([before, after], axis=1)

    for k, own, out, parts in ((0, s_own, s0, 3), (1, h_own, h0, 1)):
        x = dot_parts(sides(k), matrix, parts)
        for q in range(CELL):
            for r in range(CELL):
                y = own[q, r] + x[q * ROWS : (q + 1) * ROWS, r * LANES : (r + 1) * LANES]
                out[q, r] = y * (1.0 / DEPTH_LEVELS) if k else y

    def put(ref):
        def at(q, r, x):
            ref[q, r] = x

        return at

    last = []
    levels = (
        (8, h0, ke0, kn0, s0, d0, w0, k0, v0, it0, put(s1), put(h1)),
        (4, h1, ke1, kn1, s1, d1, w1, k1, v1, it1, put(s2), put(h2)),
        (2, h2, ke2, kn2, s2, d2, w2, k2, v2, it2, lambda q, r, x: last.append(x), lambda q, r, x: last.append(x)),
    )
    for n, h, ke, kn, source, d, w, k, v, it, put_s, put_h in levels:
        for r in range(n):
            h[n, r] = north(h[0, r])
        find_faces(n, h, ke, kn)
        for r in range(n):
            kn[0, r] = south(kn[n, r])
        find_weights(n, ke, kn, source, d, w, k, v)
        sweep(n, ke, kn, w, k, v, it)
        restrict(n, ke, kn, d, k, it, put_s)
        coarsen(n, h, put_h)
    s, h = last
    s3[0], s3[1] = s, h

    def send(to, low, blocks):
        rows = slice(0, 8) if low else slice(ROWS - 8, ROWS)
        for q in range(CELL):
            for g in range(2):
                four = []
                for r in range(4 * g, 4 * g + 4):
                    a, b = s0[q, r, rows, :], pltpu.roll(h0[q, r, rows, :], 4, 0)
                    four.append(jnp.where(row_of(a) < 4, a, b) if low else jnp.where(row_of(a) < 4, b, a))
                for i, x in enumerate(fold(four, lane_of(four[0]) >= SIDE)):
                    to[6 * q + 3 * g + i] = x
        for i, x in enumerate(blocks):
            to[6 * CELL + i] = x

    def fill(to_next, to_previous):
        send(to_next, False, (s[24:32], s[16:24], h[24:32], h[16:24]))
        send(to_previous, True, (s[0:8], s[8:16], h[0:8], h[8:16]))

    by_parity("lat", fill, out_first, out_second)


def up_kernel(
    s0_in, h0_in, s1_in, h1_in, s2_in, h2_in, s3_in, it0_in, it1_in, it2_in,
    ke0_in, kn0_in, d0_in, w0_in, k0_in, ke1_in, kn1_in, d1_in, w1_in, k1_in, ke2_in, kn2_in, d2_in, w2_in, k2_in,
    first, second, join,
    pressure, residual,
    far, s0, h0, ke0, kn0, d0, w0, k0, e0, g0, a0, b0,
    s1, h1, ke1, kn1, d1, w1, k1, e1, g1, a1, b1, s2, h2, ke2, kn2, d2, w2, k2, e2, g2, a2, b2, flat, nat, sems,
):
    def fill(high, low):
        for q in range(CELL):
            for g in range(2):
                lows = unfold([low[6 * q + 3 * g + i] for i in range(3)], 0)
                highs = unfold([high[6 * q + 3 * g + i] for i in range(3)], 0)
                for r, a, b in zip(range(4 * g, 4 * g + 4), highs, lows):
                    s_new = jnp.where(row_of(a) < 4, a, b)
                    h_new = pltpu.roll(jnp.where(row_of(a) < 4, b, a), 4, 0)
                    for to, inner, new in ((s0, s0_in, s_new), (h0, h0_in, h_new)):
                        to[q, r, 0:8, :] = inner[q, r, ROWS - 8 : ROWS, :]
                        to[q, r, 8:16, :] = new
                        to[q, r, 16:24, :] = inner[q, r, 0:8, :]
        for i in range(4):
            far[0, i] = high[6 * CELL + i]
            far[1, i] = low[6 * CELL + i]

    by_parity("lat", fill, first, second)

    levels = (
        (8, h0, ke0, kn0, s0, d0, w0, k0, e0, g0, a0, b0, (ke0_in, kn0_in, d0_in, w0_in, k0_in), it0_in),
        (4, h1, ke1, kn1, s1, d1, w1, k1, e1, g1, a1, b1, (ke1_in, kn1_in, d1_in, w1_in, k1_in), it1_in),
        (2, h2, ke2, kn2, s2, d2, w2, k2, e2, g2, a2, b2, (ke2_in, kn2_in, d2_in, w2_in, k2_in), it2_in),
    )
    source3 = []
    for i, (n, h, ke, kn, source, d, w, k, e, g, _, _, inner, _) in enumerate(levels):
        for r in range(n):
            h[n, r] = strip_of(north(Whole((h0_in, h1_in, h2_in)[i], h)[0, r]))
        find_faces(n, h, ke, kn)
        for r in range(n):
            kn[0, r] = strip_of(south(Whole(inner[1], kn)[n, r]))
        find_weights(n, ke, kn, source, d, w, k, e)
        sweep(n, ke, kn, w, k, e, g)
        if i < 2:
            s_next, s_inner, h_next = ((s1, s1_in, h1), (s2, s2_in, h2))[i]

            def put_s(q, r, x, s_next=s_next, s_inner=s_inner):
                s_next[q, r] = strip_of(merged(s_inner[q, r], x))

            def put_h(q, r, x, h_next=h_next):
                h_next[q, r] = x

            restrict(n, ke, kn, d, k, g, put_s)
            coarsen(n, h, put_h)
        else:
            restrict(n, ke, kn, d, k, g, lambda q, r, x: source3.append(x))

    strip = source3[0]
    s = merged(s3_in[0], strip)
    row = row_of(far[0, 0])
    s = jnp.concatenate(
        [
            s[0:ROWS],
            jnp.where(row < 2, strip[8:16], far[0, 0]),
            jnp.where(row < 4, far[0, 1], far[1, 1]),
            jnp.where(row >= 6, strip[8:16], far[1, 0]),
        ],
        axis=0,
    )
    h = jnp.concatenate([s3_in[1], far[0, 2], jnp.where(row < 4, far[0, 3], far[1, 3]), far[1, 2]], axis=0)
    ke, kn = jnp.minimum(h, east(h)), jnp.minimum(h, north(h))
    kw, ks = west(ke), south(kn)
    _, weight, s = weigh((ke + kw) + (kn + ks), s)
    v = weight * s
    for _ in range(COARSE_SWEEPS - 1):
        total = (ke * east(v) + kw * west(v)) + (kn * north(v) + ks * south(v))
        v = (1.0 - OMEGA) * v + weight * (s + total)
    coarse = jnp.concatenate([v[0:ROWS], jnp.where(row < 4, v[32:40], v[48:56])], axis=0)

    above = lambda q, r: coarse
    for n, _, ke, kn, _, d, w, k, _, g, a, b, inner, it in reversed(levels):
        for q in range(n):
            for r in range(n):
                a[q + 1, r] = merged(it[q + 1, r], g[q + 1, r]) + above(q // 2, r // 2)
        close(a, n)
        ke, kn, w, k = (Whole(x, y) for x, y in zip((inner[0], inner[1], inner[3], inner[4]), (ke, kn, w, k)))
        sweep(n, ke, kn, w, k, a, b)
        if n < CELL:
            sweep(n, ke, kn, w, k, b, a)
        above = lambda q, r, a=a: a[q + 1, r]

    def flatten(q, xs):
        lane = lane_of(xs[0])
        held = (lane >= LEAD) & (lane < LEAD + COLS)
        for r in range(4):
            x = jnp.where(held, xs[r], pltpu.roll(xs[r + 4], COLS, 1))
            flat[q * ROWS : (q + 1) * ROWS, r * LANES : (r + 1) * LANES] = x

    def finish(i, out):
        copies = []
        width = 2 * LANES
        for half in range(out.shape[1] // width):
            res = dot_parts(flat[...], join[:, half * width : (half + 1) * width], 2)
            for c in (2 * half, 2 * half + 1):
                at = slice((c - 2 * half) * LANES, (c - 2 * half + 1) * LANES)
                for q in range(CELL):
                    nat[i, c, pl.ds(q, ROWS, stride=CELL), :] = res[q * ROWS : (q + 1) * ROWS, at]
                copy = pltpu.make_async_copy(nat.at[i, c], out.at[:, c * LANES : (c + 1) * LANES], sems.at[i, c])
                copy.start()
                copies.append(copy)
        return copies

    sweep(8, ke, kn, w, k, b0, a0, flatten)
    copies = finish(0, pressure)
    inner = levels[0][12]
    ke, kn, d, k = (
        Whole(x, y, ROWS) for x, y in zip((inner[0], inner[1], inner[2], inner[4]), (ke0, kn0, d0, k0))
    )
    for q in range(CELL):
        flatten(q, remains(8, ke, kn, d, k, a0, q, ROWS))
    copies += finish(1, residual)
    for copy in copies:
        copy.wait()


def swap(x, axis, count, offset, closed):
    pairs = []
    for i in range(offset, count, 2):
        if i + 1 < count or closed:
            j = (i + 1) % count
            pairs += [(i, j), (j, i)]
    return lax.ppermute(x, axis, pairs)


def own_matrix(columns):
    out = np.zeros((columns, CELL * LANES), np.float32)
    c = np.arange(columns)
    out[c, (c % CELL) * LANES + LEAD + c // CELL] = 1.0
    return jnp.asarray(out, jnp.bfloat16)


def side_matrix(columns):
    out = np.zeros((2 * LANES, CELL * LANES), np.float32)
    c = np.arange(LANES - SIDE, LANES)
    out[c, (c % CELL) * LANES + LEAD + (c - LANES) // CELL] = 1.0
    c = np.arange(SIDE)
    out[LANES + c, (c % CELL) * LANES + LEAD + (columns + c) // CELL] = 1.0
    return jnp.asarray(out, jnp.bfloat16)


def join_matrix(columns):
    out = np.zeros((4 * LANES, columns), np.float32)
    c = np.arange(columns)
    r, lane = c % CELL, c // CELL + LEAD
    out[(r % 4) * LANES + np.where(r < 4, lane, (lane + COLS) % LANES), c] = 1.0
    return jnp.asarray(out, jnp.bfloat16)


VMEM = pl.BlockSpec(memory_space=pltpu.VMEM)
ANY = pl.BlockSpec(memory_space=pl.ANY)


def shaped(*dims):
    return jax.ShapeDtypeStruct(dims, jnp.float32)


def planes(n, more=0, rows=ROWS):
    return (n + more, n, rows, LANES)


def buffers(*shapes):
    return [pltpu.VMEM(s, jnp.float32) for s in shapes]


def limit(mib):
    return pltpu.CompilerParams(vmem_limit_bytes=mib * 1024 * 1024)


def cost(flops, moved):
    return pl.CostEstimate(flops=flops, bytes_accessed=moved, transcendentals=0)


def local(right_side, depth_level, ocean_mask):
    rows, columns = right_side.shape
    lon, lat = lax.axis_size("lon"), lax.axis_size("lat")
    side = pltpu.VMEM((2, rows, LANES), jnp.float32), pltpu.VMEM((2, rows, LANES), jnp.int32)
    first, second = pl.pallas_call(
        pack_kernel,
        out_shape=[shaped(2, 3 * rows // 4, LANES)] * 2,
        in_specs=[ANY] * 3,
        out_specs=[VMEM] * 2,
        scratch_shapes=[side[0], side[1], side[1], pltpu.SemaphoreType.DMA((2, 3))],
        compiler_params=limit(58),
    )(right_side, depth_level, ocean_mask)
    first = swap(first, "lon", lon, 0, True)
    second = swap(second, "lon", lon, 1, True)
    tiles = (columns // LANES, rows, LANES)
    own = pl.pallas_call(
        own_kernel,
        out_shape=[shaped(*planes(8))] * 2,
        in_specs=[VMEM] * 4,
        out_specs=[VMEM] * 2,
        scratch_shapes=buffers(tiles, tiles),
        compiler_params=limit(16),
        cost_estimate=cost(8 * rows * columns * CELL * LANES, 16 * rows * columns),
    )(right_side, depth_level, ocean_mask, own_matrix(columns))

    message = shaped(6 * CELL + 4, 8, LANES)
    levels = (8, 4, 2)
    coefficients = [s for n in levels for s in (planes(n), planes(n, 1), planes(n), planes(n), planes(n))]
    fields = [s for n in levels for s in (planes(n), planes(n, 1))] + [(2, ROWS, LANES)] + [planes(n, 2) for n in levels]
    *fields, first, second = pl.pallas_call(
        down_kernel,
        out_shape=[shaped(*s) for s in fields + coefficients] + [message] * 2,
        in_specs=[VMEM] * 5,
        out_specs=[VMEM] * (len(fields) + len(coefficients) + 2),
        scratch_shapes=buffers(*[planes(n, 2) for n in levels]),
        compiler_params=limit(24),
    )(first, second, *own, side_matrix(columns))
    first = swap(first, "lat", lat, 0, False)
    second = swap(second, "lat", lat, 1, False)
    return pl.pallas_call(
        up_kernel,
        out_shape=[shaped(rows, columns)] * 2,
        in_specs=[VMEM] * (len(fields) + 3),
        out_specs=[ANY] * 2,
        scratch_shapes=buffers(
            (2, 4, 8, LANES),
            *[
                s
                for n in levels
                for s in (
                    planes(n, 0, 24), planes(n, 1, 24), planes(n, 0, 24), planes(n, 1, 24),
                    planes(n, 0, 24), planes(n, 0, 24), planes(n, 0, 24),
                    planes(n, 2, 24), planes(n, 2, 24), planes(n, 2, TALL), planes(n, 2, TALL),
                )
            ],
            (rows, 4 * LANES), (2, *tiles),
        ) + [pltpu.SemaphoreType.DMA((2, columns // LANES))],
        compiler_params=limit(24),
    )(*fields, first, second, join_matrix(columns))


def solution(mesh):
    placed = (P("lat", "lon"), P("lat", "lon"), P("lat", "lon"))
    return jax.shard_map(
        local,
        mesh=mesh,
        in_specs=placed,
        out_specs=(P("lat", "lon"), P("lat", "lon")),
        check_vma=False,
    )
```

```python
import jax
import jax.numpy as jnp
import numpy as np
from jax import lax
from jax.experimental import pallas as pl
from jax.experimental.pallas import tpu as pltpu
from jax.sharding import PartitionSpec as P

LEVELS = 4
COARSE_SWEEPS = 9
DEPTH_LEVELS = 50
OMEGA = 0.8
SIGMA = 1e-05

CELL = 2 ** (LEVELS - 1)
LANES = 128
SIDE = 96
LEAD = 16
ROWS = 32
COLS = 64
TALL = ROWS + 8


def east(x):
    return pltpu.roll(x, x.shape[1] - 1, 1)


def west(x):
    return pltpu.roll(x, 1, 1)


def north(x):
    return pltpu.roll(x, x.shape[0] - 1, 0)


def south(x):
    return pltpu.roll(x, 1, 0)


def row_of(x):
    return lax.broadcasted_iota(jnp.int32, x.shape, 0)


def lane_of(x):
    return lax.broadcasted_iota(jnp.int32, x.shape, 1)


class Whole:
    def __init__(self, inner, strip, count=TALL):
        self.inner, self.strip, self.count = inner, strip, count

    def __getitem__(self, at):
        q, r = at
        parts = [self.strip[q, r, 16:24, :], self.inner[q, r, 8:24, :], self.strip[q, r, 0 : self.count - 24, :]]
        return jnp.concatenate(parts, axis=0)


def strip_of(x):
    return jnp.concatenate([x[24:TALL], x[0:8]], axis=0)


def merged(inner, strip):
    low = jnp.where(row_of(strip[0:8]) < 2, strip[16:24], inner[0:8])
    high = jnp.where(row_of(strip[0:8]) >= 6, strip[0:8], inner[24:32])
    return jnp.concatenate([low, inner[8:24], high, strip[8:16]], axis=0)


def close(v, n):
    for r in range(n):
        v[0, r] = south(v[n, r])
        v[n + 1, r] = north(v[1, r])


def find_faces(n, h, ke, kn):
    for q in range(n):
        for r in range(n):
            here = h[q, r]
            ke[q, r] = jnp.minimum(here, h[q, r + 1] if r + 1 < n else east(h[q, 0]))
            kn[q + 1, r] = jnp.minimum(here, h[q + 1, r])


def weigh(faces, source):
    diagonal = SIGMA + faces
    return diagonal, OMEGA / diagonal, jnp.where(faces > 0.0, source, 0.0)


def find_weights(n, ke, kn, source, d, w, s, v):
    for q in range(n):
        for r in range(n):
            kw = ke[q, r - 1] if r else west(ke[q, n - 1])
            faces = (ke[q, r] + kw) + (kn[q + 1, r] + kn[q, r])
            diagonal, weight, kept = weigh(faces, source[q, r])
            d[q, r], w[q, r], s[q, r] = diagonal, weight, kept
            v[q + 1, r] = weight * kept
    close(v, n)


def pull(n, ke, kn, v, q, count=None):
    ks = [ke[q, r] for r in range(n)]
    cs = [v[q + 1, r][:count] for r in range(n)]
    out = []
    for r in range(n):
        kw = ks[r - 1] if r else west(ks[n - 1])
        ve = cs[r + 1] if r + 1 < n else east(cs[0])
        vw = cs[r - 1] if r else west(cs[n - 1])
        out.append((ks[r] * ve + kw * vw) + (kn[q + 1, r] * v[q + 2, r][:count] + kn[q, r] * v[q, r][:count]))
    return cs, out


def sweep(n, ke, kn, w, s, v, out, also=None):
    for q in range(n):
        cs, total = pull(n, ke, kn, v, q)
        for r in range(n):
            new = (1.0 - OMEGA) * cs[r] + w[q, r] * (s[q, r] + total[r])
            out[q + 1, r] = new
        if also is not None:
            also(q, [out[q + 1, r][:ROWS] for r in range(n)])
    close(out, n)


def remains(n, ke, kn, d, s, v, q, count=None):
    cs, total = pull(n, ke, kn, v, q, count)
    return [(s[q, r] - d[q, r] * cs[r]) + total[r] for r in range(n)]


def restrict(n, ke, kn, d, s, v, put):
    for q in range(n // 2):
        a = remains(n, ke, kn, d, s, v, 2 * q)
        b = remains(n, ke, kn, d, s, v, 2 * q + 1)
        for r in range(n // 2):
            put(q, r, 0.25 * ((a[2 * r] + a[2 * r + 1]) + (b[2 * r] + b[2 * r + 1])))


def coarsen(n, h, put):
    for q in range(n // 2):
        for r in range(n // 2):
            a = h[2 * q, 2 * r] + h[2 * q, 2 * r + 1]
            b = h[2 * q + 1, 2 * r] + h[2 * q + 1, 2 * r + 1]
            put(q, r, 0.0625 * (a + b))


def dot_parts(x, matrix, parts):
    out = 0.0
    for part in range(parts):
        piece = x.astype(jnp.bfloat16)
        out = out + jnp.dot(piece, matrix, preferred_element_type=jnp.float32)
        if part + 1 < parts:
            x = x - piece.astype(jnp.float32)
    return out


def fold(blocks, free):
    return [jnp.where(free, pltpu.roll(blocks[3], 96 - 32 * i, 1), blocks[i]) for i in range(3)]


def unfold(three, first):
    lane = lane_of(three[0])
    a, b, c = (pltpu.roll(x, 32 * (i + 1), 1) for i, x in enumerate(three))
    return list(three) + [jnp.where(lane < first + 32, a, jnp.where(lane < first + 64, b, c))]


def by_parity(axis, fill, first, second):
    even = lax.rem(lax.axis_index(axis), 2) == 0

    @pl.when(even)
    def _():
        fill(first, second)

    @pl.when(jnp.logical_not(even))
    def _():
        fill(second, first)


def pack_kernel(f, depth, mask, first, second, fs, ds, ms, sems):
    last = f.shape[1] - LANES
    copies = []
    for j, column in enumerate((0, last)):
        for i, (source, to) in enumerate(((f, fs), (depth, ds), (mask, ms))):
            copies.append(pltpu.make_async_copy(source.at[:, column : column + LANES], to.at[j], sems.at[j, i]))
    for copy in copies:
        copy.start()
    for copy in copies:
        copy.wait()

    def fill(to_next, to_previous):
        for j, to in enumerate((to_previous, to_next)):
            count = ROWS * CELL // 4
            s_blocks, h_blocks = [], []
            for block in range(4):
                s_rows, h_rows = [], []
                for q in (2 * block, 2 * block + 1):
                    rows = pl.ds(q, ROWS, stride=CELL)
                    s_rows.append(fs[j, rows, :])
                    h_rows.append((ds[j, rows, :] * ms[j, rows, :]).astype(jnp.float32))
                s_blocks.append(jnp.concatenate(s_rows, axis=0))
                h_blocks.append(jnp.concatenate(h_rows, axis=0))
            lane = lane_of(s_blocks[0])
            free = lane < LANES - SIDE if j else lane >= SIDE
            for k, blocks in enumerate((s_blocks, h_blocks)):
                for i, x in enumerate(fold(blocks, free)):
                    to[k, i * count : (i + 1) * count, :] = x

    by_parity("lon", fill, first, second)


def own_kernel(f, depth, mask, s0, h0, nat_s, nat_h):
    lane = lax.broadcasted_iota(jnp.int32, (1, CELL * LANES), 1)
    column = CELL * ((lane & (LANES - 1)) - LEAD) + lane // LANES
    row = lax.broadcasted_iota(jnp.int32, (f.shape[1], CELL * LANES), 0)
    matrix = jnp.where(row == column, 1.0, 0.0).astype(jnp.bfloat16)
    tiles = nat_s.shape[0]
    for c in range(tiles):
        lanes = slice(c * LANES, (c + 1) * LANES)
        nat_s[c] = f[:, lanes]
        nat_h[c] = (depth[:, lanes] * mask[:, lanes]).astype(jnp.float32)
    for nat, out, parts in ((nat_s, s0, 3), (nat_h, h0, 1)):
        rows = [
            jnp.concatenate([nat[c, pl.ds(q, ROWS, stride=CELL), :] for c in range(tiles)], axis=1) for q in range(CELL)
        ]
        x = dot_parts(jnp.concatenate(rows, axis=0), matrix, parts)
        for q in range(CELL):
            for r in range(CELL):
                out[q, r] = x[q * ROWS : (q + 1) * ROWS, r * LANES : (r + 1) * LANES]


def down_kernel(
    first, second, s_own, h_own, split,
    s0, h0, s1, h1, s2, h2, s3, it0, it1, it2,
    ke0, kn0, d0, w0, k0, ke1, kn1, d1, w1, k1, ke2, kn2, d2, w2, k2, out_second, out_first,
    v0, v1, v2,
):
    even = lax.rem(lax.axis_index("lon"), 2) == 0
    matrix = split[...]
    count = ROWS * CELL // 4

    def sides(k):
        before, after = [], []
        for i in range(3):
            rows = slice(i * count, (i + 1) * count)
            a, b = first[k, rows, :], second[k, rows, :]
            before.append(jnp.where(even, b, a))
            after.append(jnp.where(even, a, b))
        before = jnp.concatenate(unfold(before, LANES - SIDE), axis=0)
        after = jnp.concatenate(unfold(after, 0), axis=0)
        return jnp.concatenate([before, after], axis=1)

    for k, own, out, parts in ((0, s_own, s0, 3), (1, h_own, h0, 1)):
        x = dot_parts(sides(k), matrix, parts)
        for q in range(CELL):
            for r in range(CELL):
                y = own[q, r] + x[q * ROWS : (q + 1) * ROWS, r * LANES : (r + 1) * LANES]
                out[q, r] = y * (1.0 / DEPTH_LEVELS) if k else y

    def put(ref):
        def at(q, r, x):
            ref[q, r] = x

        return at

    last = []
    levels = (
        (8, h0, ke0, kn0, s0, d0, w0, k0, v0, it0, put(s1), put(h1)),
        (4, h1, ke1, kn1, s1, d1, w1, k1, v1, it1, put(s2), put(h2)),
        (2, h2, ke2, kn2, s2, d2, w2, k2, v2, it2, lambda q, r, x: last.append(x), lambda q, r, x: last.append(x)),
    )
    for n, h, ke, kn, source, d, w, k, v, it, put_s, put_h in levels:
        for r in range(n):
            h[n, r] = north(h[0, r])
        find_faces(n, h, ke, kn)
        for r in range(n):
            kn[0, r] = south(kn[n, r])
        find_weights(n, ke, kn, source, d, w, k, v)
        sweep(n, ke, kn, w, k, v, it)
        restrict(n, ke, kn, d, k, it, put_s)
        coarsen(n, h, put_h)
    s, h = last
    s3[0], s3[1] = s, h

    def send(to, low, blocks):
        rows = slice(0, 8) if low else slice(ROWS - 8, ROWS)
        for q in range(CELL):
            for g in range(2):
                four = []
                for r in range(4 * g, 4 * g + 4):
                    a, b = s0[q, r, rows, :], pltpu.roll(h0[q, r, rows, :], 4, 0)
                    four.append(jnp.where(row_of(a) < 4, a, b) if low else jnp.where(row_of(a) < 4, b, a))
                for i, x in enumerate(fold(four, lane_of(four[0]) >= SIDE)):
                    to[6 * q + 3 * g + i] = x
        for i, x in enumerate(blocks):
            to[6 * CELL + i] = x

    def fill(to_next, to_previous):
        send(to_next, False, (s[24:32], s[16:24], h[24:32], h[16:24]))
        send(to_previous, True, (s[0:8], s[8:16], h[0:8], h[8:16]))

    by_parity("lat", fill, out_first, out_second)


def up_kernel(
    s0_in, h0_in, s1_in, h1_in, s2_in, h2_in, s3_in, it0_in, it1_in, it2_in,
    ke0_in, kn0_in, d0_in, w0_in, k0_in, ke1_in, kn1_in, d1_in, w1_in, k1_in, ke2_in, kn2_in, d2_in, w2_in, k2_in,
    second, first, join,
    pressure, residual,
    far, s0, h0, ke0, kn0, d0, w0, k0, e0, g0, a0, b0,
    s1, h1, ke1, kn1, d1, w1, k1, e1, g1, a1, b1, s2, h2, ke2, kn2, d2, w2, k2, e2, g2, a2, b2, flat, nat, sems,
):
    def fill(high, low):
        for q in range(CELL):
            for g in range(2):
                lows = unfold([low[6 * q + 3 * g + i] for i in range(3)], 0)
                highs = unfold([high[6 * q + 3 * g + i] for i in range(3)], 0)
                for r, a, b in zip(range(4 * g, 4 * g + 4), highs, lows):
                    s_new = jnp.where(row_of(a) < 4, a, b)
                    h_new = pltpu.roll(jnp.where(row_of(a) < 4, b, a), 4, 0)
                    for to, inner, new in ((s0, s0_in, s_new), (h0, h0_in, h_new)):
                        to[q, r, 0:8, :] = inner[q, r, ROWS - 8 : ROWS, :]
                        to[q, r, 8:16, :] = new
                        to[q, r, 16:24, :] = inner[q, r, 0:8, :]
        for i in range(4):
            far[0, i] = high[6 * CELL + i]
            far[1, i] = low[6 * CELL + i]

    by_parity("lat", fill, first, second)

    levels = (
        (8, h0, ke0, kn0, s0, d0, w0, k0, e0, g0, a0, b0, (ke0_in, kn0_in, d0_in, w0_in, k0_in), it0_in),
        (4, h1, ke1, kn1, s1, d1, w1, k1, e1, g1, a1, b1, (ke1_in, kn1_in, d1_in, w1_in, k1_in), it1_in),
        (2, h2, ke2, kn2, s2, d2, w2, k2, e2, g2, a2, b2, (ke2_in, kn2_in, d2_in, w2_in, k2_in), it2_in),
    )
    source3 = []
    for i, (n, h, ke, kn, source, d, w, k, e, g, _, _, inner, _) in enumerate(levels):
        for r in range(n):
            h[n, r] = strip_of(north(Whole((h0_in, h1_in, h2_in)[i], h)[0, r]))
        find_faces(n, h, ke, kn)
        for r in range(n):
            kn[0, r] = strip_of(south(Whole(inner[1], kn)[n, r]))
        find_weights(n, ke, kn, source, d, w, k, e)
        sweep(n, ke, kn, w, k, e, g)
        if i < 2:
            s_next, s_inner, h_next = ((s1, s1_in, h1), (s2, s2_in, h2))[i]

            def put_s(q, r, x, s_next=s_next, s_inner=s_inner):
                s_next[q, r] = strip_of(merged(s_inner[q, r], x))

            def put_h(q, r, x, h_next=h_next):
                h_next[q, r] = x

            restrict(n, ke, kn, d, k, g, put_s)
            coarsen(n, h, put_h)
        else:
            restrict(n, ke, kn, d, k, g, lambda q, r, x: source3.append(x))

    strip = source3[0]
    s = merged(s3_in[0], strip)
    row = row_of(far[0, 0])
    s = jnp.concatenate(
        [
            s[0:ROWS],
            jnp.where(row < 2, strip[8:16], far[0, 0]),
            jnp.where(row < 4, far[0, 1], far[1, 1]),
            jnp.where(row >= 6, strip[8:16], far[1, 0]),
        ],
        axis=0,
    )
    h = jnp.concatenate([s3_in[1], far[0, 2], jnp.where(row < 4, far[0, 3], far[1, 3]), far[1, 2]], axis=0)
    ke, kn = jnp.minimum(h, east(h)), jnp.minimum(h, north(h))
    kw, ks = west(ke), south(kn)
    _, weight, s = weigh((ke + kw) + (kn + ks), s)
    v = weight * s
    for _ in range(COARSE_SWEEPS - 1):
        total = (ke * east(v) + kw * west(v)) + (kn * north(v) + ks * south(v))
        v = (1.0 - OMEGA) * v + weight * (s + total)
    coarse = jnp.concatenate([v[0:ROWS], jnp.where(row < 4, v[32:40], v[48:56])], axis=0)

    above = lambda q, r: coarse
    for n, _, ke, kn, _, d, w, k, _, g, a, b, inner, it in reversed(levels):
        for q in range(n):
            for r in range(n):
                a[q + 1, r] = merged(it[q + 1, r], g[q + 1, r]) + above(q // 2, r // 2)
        close(a, n)
        ke, kn, w, k = (Whole(x, y) for x, y in zip((inner[0], inner[1], inner[3], inner[4]), (ke, kn, w, k)))
        sweep(n, ke, kn, w, k, a, b)
        if n < CELL:
            sweep(n, ke, kn, w, k, b, a)
        above = lambda q, r, a=a: a[q + 1, r]

    def flatten(q, xs):
        lane = lane_of(xs[0])
        held = (lane >= LEAD) & (lane < LEAD + COLS)
        for r in range(4):
            x = jnp.where(held, xs[r], pltpu.roll(xs[r + 4], COLS, 1))
            flat[q * ROWS : (q + 1) * ROWS, r * LANES : (r + 1) * LANES] = x

    def finish(i, out):
        copies = []
        width = 2 * LANES
        for half in range(out.shape[1] // width):
            res = dot_parts(flat[...], join[:, half * width : (half + 1) * width], 2)
            for c in (2 * half, 2 * half + 1):
                at = slice((c - 2 * half) * LANES, (c - 2 * half + 1) * LANES)
                for q in range(CELL):
                    nat[i, c, pl.ds(q, ROWS, stride=CELL), :] = res[q * ROWS : (q + 1) * ROWS, at]
                copy = pltpu.make_async_copy(nat.at[i, c], out.at[:, c * LANES : (c + 1) * LANES], sems.at[i, c])
                copy.start()
                copies.append(copy)
        return copies

    sweep(8, ke, kn, w, k, b0, a0, flatten)
    copies = finish(0, pressure)
    inner = levels[0][12]
    ke, kn, d, k = (
        Whole(x, y, ROWS) for x, y in zip((inner[0], inner[1], inner[2], inner[4]), (ke0, kn0, d0, k0))
    )
    for q in range(CELL):
        flatten(q, remains(8, ke, kn, d, k, a0, q, ROWS))
    copies += finish(1, residual)
    for copy in copies:
        copy.wait()


def swap(x, axis, count, offset, closed):
    pairs = []
    for i in range(offset, count, 2):
        if i + 1 < count or closed:
            j = (i + 1) % count
            pairs += [(i, j), (j, i)]
    return lax.ppermute(x, axis, pairs)


def side_matrix(columns):
    out = np.zeros((2 * LANES, CELL * LANES), np.float32)
    c = np.arange(LANES - SIDE, LANES)
    out[c, (c % CELL) * LANES + LEAD + (c - LANES) // CELL] = 1.0
    c = np.arange(SIDE)
    out[LANES + c, (c % CELL) * LANES + LEAD + (columns + c) // CELL] = 1.0
    return jnp.asarray(out, jnp.bfloat16)


def join_matrix(columns):
    out = np.zeros((4 * LANES, columns), np.float32)
    c = np.arange(columns)
    r, lane = c % CELL, c // CELL + LEAD
    out[(r % 4) * LANES + np.where(r < 4, lane, (lane + COLS) % LANES), c] = 1.0
    return jnp.asarray(out, jnp.bfloat16)


VMEM = pl.BlockSpec(memory_space=pltpu.VMEM)
ANY = pl.BlockSpec(memory_space=pl.ANY)


def shaped(*dims):
    return jax.ShapeDtypeStruct(dims, jnp.float32)


def planes(n, more=0, rows=ROWS):
    return (n + more, n, rows, LANES)


def buffers(*shapes):
    return [pltpu.VMEM(s, jnp.float32) for s in shapes]


def limit(mib):
    return pltpu.CompilerParams(vmem_limit_bytes=mib * 1024 * 1024)


def cost(flops, moved):
    return pl.CostEstimate(flops=flops, bytes_accessed=moved, transcendentals=0)


def local(right_side, depth_level, ocean_mask):
    rows, columns = right_side.shape
    lon, lat = lax.axis_size("lon"), lax.axis_size("lat")
    side = pltpu.VMEM((2, rows, LANES), jnp.float32), pltpu.VMEM((2, rows, LANES), jnp.int32)
    first, second = pl.pallas_call(
        pack_kernel,
        out_shape=[shaped(2, 3 * rows // 4, LANES)] * 2,
        in_specs=[ANY] * 3,
        out_specs=[VMEM] * 2,
        scratch_shapes=[side[0], side[1], side[1], pltpu.SemaphoreType.DMA((2, 3))],
        compiler_params=limit(58),
    )(right_side, depth_level, ocean_mask)
    first = swap(first, "lon", lon, 0, True)
    second = swap(second, "lon", lon, 1, True)
    tiles = (columns // LANES, rows, LANES)
    own = pl.pallas_call(
        own_kernel,
        out_shape=[shaped(*planes(8))] * 2,
        in_specs=[VMEM] * 3,
        out_specs=[VMEM] * 2,
        scratch_shapes=buffers(tiles, tiles),
        compiler_params=limit(16),
        cost_estimate=cost(8 * rows * columns * CELL * LANES, 16 * rows * columns),
    )(right_side, depth_level, ocean_mask)

    message = shaped(6 * CELL + 4, 8, LANES)
    levels = (8, 4, 2)
    coefficients = [s for n in levels for s in (planes(n), planes(n, 1), planes(n), planes(n), planes(n))]
    fields = [s for n in levels for s in (planes(n), planes(n, 1))] + [(2, ROWS, LANES)] + [planes(n, 2) for n in levels]
    *fields, second, first = pl.pallas_call(
        down_kernel,
        out_shape=[shaped(*s) for s in fields + coefficients] + [message] * 2,
        in_specs=[VMEM] * 5,
        out_specs=[VMEM] * (len(fields) + len(coefficients) + 2),
        scratch_shapes=buffers(*[planes(n, 2) for n in levels]),
        compiler_params=limit(24),
    )(first, second, *own, side_matrix(columns))
    second = swap(second, "lat", lat, 1, False)
    first = swap(first, "lat", lat, 0, False)
    return pl.pallas_call(
        up_kernel,
        out_shape=[shaped(rows, columns)] * 2,
        in_specs=[VMEM] * (len(fields) + 3),
        out_specs=[ANY] * 2,
        scratch_shapes=buffers(
            (2, 4, 8, LANES),
            *[
                s
                for n in levels
                for s in (
                    planes(n, 0, 24), planes(n, 1, 24), planes(n, 0, 24), planes(n, 1, 24),
                    planes(n, 0, 24), planes(n, 0, 24), planes(n, 0, 24),
                    planes(n, 2, 24), planes(n, 2, 24), planes(n, 2, TALL), planes(n, 2, TALL),
                )
            ],
            (rows, 4 * LANES), (2, *tiles),
        ) + [pltpu.SemaphoreType.DMA((2, columns // LANES))],
        compiler_params=limit(24),
    )(*fields, second, first, join_matrix(columns))


def solution(mesh):
    placed = (P("lat", "lon"), P("lat", "lon"), P("lat", "lon"))
    return jax.shard_map(
        local,
        mesh=mesh,
        in_specs=placed,
        out_specs=(P("lat", "lon"), P("lat", "lon")),
        check_vma=False,
    )
```

```python
import jax
import jax.numpy as jnp
import numpy as np
from jax import lax
from jax.experimental import pallas as pl
from jax.experimental.pallas import tpu as pltpu
from jax.sharding import PartitionSpec as P

LEVELS = 4
COARSE_SWEEPS = 9
DEPTH_LEVELS = 50
OMEGA = 0.8
SIGMA = 1e-05

CELL = 2 ** (LEVELS - 1)
LANES = 128
SIDE = 96
LEAD = 16
ROWS = 32
COLS = 64
TALL = ROWS + 8


def east(x):
    return pltpu.roll(x, x.shape[1] - 1, 1)


def west(x):
    return pltpu.roll(x, 1, 1)


def north(x):
    return pltpu.roll(x, x.shape[0] - 1, 0)


def south(x):
    return pltpu.roll(x, 1, 0)


def row_of(x):
    return lax.broadcasted_iota(jnp.int32, x.shape, 0)


def lane_of(x):
    return lax.broadcasted_iota(jnp.int32, x.shape, 1)


class Whole:
    def __init__(self, inner, strip, count=TALL):
        self.inner, self.strip, self.count = inner, strip, count

    def __getitem__(self, at):
        q, r = at
        parts = [self.strip[q, r, 16:24, :], self.inner[q, r, 8:24, :], self.strip[q, r, 0 : self.count - 24, :]]
        return jnp.concatenate(parts, axis=0)


def strip_of(x):
    return jnp.concatenate([x[24:TALL], x[0:8]], axis=0)


def merged(inner, strip):
    low = jnp.where(row_of(strip[0:8]) < 2, strip[16:24], inner[0:8])
    high = jnp.where(row_of(strip[0:8]) >= 6, strip[0:8], inner[24:32])
    return jnp.concatenate([low, inner[8:24], high, strip[8:16]], axis=0)


def close(v, n):
    for r in range(n):
        v[0, r] = south(v[n, r])
        v[n + 1, r] = north(v[1, r])


def find_faces(n, h, ke, kn):
    for q in range(n):
        for r in range(n):
            here = h[q, r]
            ke[q, r] = jnp.minimum(here, h[q, r + 1] if r + 1 < n else east(h[q, 0]))
            kn[q + 1, r] = jnp.minimum(here, h[q + 1, r])


def weigh(faces, source):
    diagonal = SIGMA + faces
    return diagonal, OMEGA * pl.reciprocal(diagonal), jnp.where(faces > 0.0, source, 0.0)


def find_weights(n, ke, kn, source, d, w, s, v):
    for q in range(n):
        for r in range(n):
            kw = ke[q, r - 1] if r else west(ke[q, n - 1])
            faces = (ke[q, r] + kw) + (kn[q + 1, r] + kn[q, r])
            diagonal, weight, kept = weigh(faces, source[q, r])
            d[q, r], w[q, r], s[q, r] = diagonal, weight, kept
            v[q + 1, r] = weight * kept
    close(v, n)


def pull(n, ke, kn, v, q, count=None):
    ks = [ke[q, r] for r in range(n)]
    cs = [v[q + 1, r][:count] for r in range(n)]
    out = []
    for r in range(n):
        kw = ks[r - 1] if r else west(ks[n - 1])
        ve = cs[r + 1] if r + 1 < n else east(cs[0])
        vw = cs[r - 1] if r else west(cs[n - 1])
        out.append((ks[r] * ve + kw * vw) + (kn[q + 1, r] * v[q + 2, r][:count] + kn[q, r] * v[q, r][:count]))
    return cs, out


def sweep(n, ke, kn, w, s, v, out, also=None, final=False):
    for q in range(n):
        cs, total = pull(n, ke, kn, v, q)
        for r in range(n):
            new = (1.0 - OMEGA) * cs[r] + w[q, r] * (s[q, r] + total[r])
            out[q + 1, r] = new
        if also is not None:
            also(q, [out[q + 1, r][:ROWS] for r in range(n)])
    if not final:
        close(out, n)


def remains(n, ke, kn, d, s, v, q, count=None):
    cs, total = pull(n, ke, kn, v, q, count)
    return [(s[q, r] - d[q, r] * cs[r]) + total[r] for r in range(n)]


def restrict(n, ke, kn, d, s, v, put):
    for q in range(n // 2):
        a = remains(n, ke, kn, d, s, v, 2 * q)
        b = remains(n, ke, kn, d, s, v, 2 * q + 1)
        for r in range(n // 2):
            put(q, r, 0.25 * ((a[2 * r] + a[2 * r + 1]) + (b[2 * r] + b[2 * r + 1])))


def coarsen(n, h, put):
    for q in range(n // 2):
        for r in range(n // 2):
            a = h[2 * q, 2 * r] + h[2 * q, 2 * r + 1]
            b = h[2 * q + 1, 2 * r] + h[2 * q + 1, 2 * r + 1]
            put(q, r, 0.0625 * (a + b))


def dot_parts(x, matrix, parts):
    out = 0.0
    for part in range(parts):
        piece = x.astype(jnp.bfloat16)
        out = out + jnp.dot(piece, matrix, preferred_element_type=jnp.float32)
        if part + 1 < parts:
            x = x - piece.astype(jnp.float32)
    return out


def fold(blocks, free):
    return [jnp.where(free, pltpu.roll(blocks[3], 96 - 32 * i, 1), blocks[i]) for i in range(3)]


def unfold(three, first):
    lane = lane_of(three[0])
    a, b, c = (pltpu.roll(x, 32 * (i + 1), 1) for i, x in enumerate(three))
    return list(three) + [jnp.where(lane < first + 32, a, jnp.where(lane < first + 64, b, c))]


def by_parity(axis, fill, first, second):
    even = lax.rem(lax.axis_index(axis), 2) == 0

    @pl.when(even)
    def _():
        fill(first, second)

    @pl.when(jnp.logical_not(even))
    def _():
        fill(second, first)


def pack_kernel(f, depth, mask, first, second, fs, ds, ms, sems):
    last = f.shape[1] - LANES
    copies = []
    for j, column in enumerate((0, last)):
        for i, (source, to) in enumerate(((f, fs), (depth, ds), (mask, ms))):
            copies.append(pltpu.make_async_copy(source.at[:, column : column + LANES], to.at[j], sems.at[j, i]))
    for copy in copies:
        copy.start()
    for copy in copies:
        copy.wait()

    def fill(to_next, to_previous):
        for j, to in enumerate((to_previous, to_next)):
            count = ROWS * CELL // 4
            s_blocks, h_blocks = [], []
            for block in range(4):
                s_rows, h_rows = [], []
                for q in (2 * block, 2 * block + 1):
                    rows = pl.ds(q, ROWS, stride=CELL)
                    s_rows.append(fs[j, rows, :])
                    h_rows.append((ds[j, rows, :] * ms[j, rows, :]).astype(jnp.float32))
                s_blocks.append(jnp.concatenate(s_rows, axis=0))
                h_blocks.append(jnp.concatenate(h_rows, axis=0))
            lane = lane_of(s_blocks[0])
            free = lane < LANES - SIDE if j else lane >= SIDE
            for k, blocks in enumerate((s_blocks, h_blocks)):
                for i, x in enumerate(fold(blocks, free)):
                    to[k, i * count : (i + 1) * count, :] = x

    by_parity("lon", fill, first, second)


def own_kernel(f, depth, mask, s0, h0, nat_s, nat_h):
    lane = lax.broadcasted_iota(jnp.int32, (1, CELL * LANES), 1)
    column = CELL * ((lane & (LANES - 1)) - LEAD) + lane // LANES
    row = lax.broadcasted_iota(jnp.int32, (f.shape[1], CELL * LANES), 0)
    matrix = jnp.where(row == column, 1.0, 0.0).astype(jnp.bfloat16)
    tiles = nat_s.shape[0]
    for c in range(tiles):
        lanes = slice(c * LANES, (c + 1) * LANES)
        nat_s[c] = f[:, lanes]
        nat_h[c] = (depth[:, lanes] * mask[:, lanes]).astype(jnp.float32)
    for nat, out, parts in ((nat_s, s0, 3), (nat_h, h0, 1)):
        rows = [
            jnp.concatenate([nat[c, pl.ds(q, ROWS, stride=CELL), :] for c in range(tiles)], axis=1) for q in range(CELL)
        ]
        x = dot_parts(jnp.concatenate(rows, axis=0), matrix, parts)
        for q in range(CELL):
            for r in range(CELL):
                out[q, r] = x[q * ROWS : (q + 1) * ROWS, r * LANES : (r + 1) * LANES]


def down_kernel(
    first, second, s_own, h_own, split,
    s0, h0, s1, h1, s2, h2, s3, it0, it1, it2,
    ke0, kn0, d0, w0, k0, ke1, kn1, d1, w1, k1, ke2, kn2, d2, w2, k2, out_second, out_first,
    v0, v1, v2,
):
    even = lax.rem(lax.axis_index("lon"), 2) == 0
    matrix = split[...]
    count = ROWS * CELL // 4

    def sides(k):
        before, after = [], []
        for i in range(3):
            rows = slice(i * count, (i + 1) * count)
            a, b = first[k, rows, :], second[k, rows, :]
            before.append(jnp.where(even, b, a))
            after.append(jnp.where(even, a, b))
        before = jnp.concatenate(unfold(before, LANES - SIDE), axis=0)
        after = jnp.concatenate(unfold(after, 0), axis=0)
        return jnp.concatenate([before, after], axis=1)

    for k, own, out, parts in ((0, s_own, s0, 3), (1, h_own, h0, 1)):
        x = dot_parts(sides(k), matrix, parts)
        for q in range(CELL):
            for r in range(CELL):
                y = own[q, r] + x[q * ROWS : (q + 1) * ROWS, r * LANES : (r + 1) * LANES]
                out[q, r] = y * (1.0 / DEPTH_LEVELS) if k else y

    def put(ref):
        def at(q, r, x):
            ref[q, r] = x

        return at

    last = []
    levels = (
        (8, h0, ke0, kn0, s0, d0, w0, k0, v0, it0, put(s1), put(h1)),
        (4, h1, ke1, kn1, s1, d1, w1, k1, v1, it1, put(s2), put(h2)),
        (2, h2, ke2, kn2, s2, d2, w2, k2, v2, it2, lambda q, r, x: last.append(x), lambda q, r, x: last.append(x)),
    )
    for n, h, ke, kn, source, d, w, k, v, it, put_s, put_h in levels:
        for r in range(n):
            h[n, r] = north(h[0, r])
        find_faces(n, h, ke, kn)
        for r in range(n):
            kn[0, r] = south(kn[n, r])
        find_weights(n, ke, kn, source, d, w, k, v)
        sweep(n, ke, kn, w, k, v, it)
        restrict(n, ke, kn, d, k, it, put_s)
        coarsen(n, h, put_h)
    s, h = last
    s3[0], s3[1] = s, h

    def send(to, low, blocks):
        rows = slice(0, 8) if low else slice(ROWS - 8, ROWS)
        for q in range(CELL):
            for g in range(2):
                four = []
                for r in range(4 * g, 4 * g + 4):
                    a, b = s0[q, r, rows, :], pltpu.roll(h0[q, r, rows, :], 4, 0)
                    four.append(jnp.where(row_of(a) < 4, a, b) if low else jnp.where(row_of(a) < 4, b, a))
                for i, x in enumerate(fold(four, lane_of(four[0]) >= SIDE)):
                    to[6 * q + 3 * g + i] = x
        for i, x in enumerate(blocks):
            to[6 * CELL + i] = x

    def fill(to_next, to_previous):
        send(to_next, False, (s[24:32], s[16:24], h[24:32], h[16:24]))
        send(to_previous, True, (s[0:8], s[8:16], h[0:8], h[8:16]))

    by_parity("lat", fill, out_first, out_second)


def up_kernel(
    s0_in, h0_in, s1_in, h1_in, s2_in, h2_in, s3_in, it0_in, it1_in, it2_in,
    ke0_in, kn0_in, d0_in, w0_in, k0_in, ke1_in, kn1_in, d1_in, w1_in, k1_in, ke2_in, kn2_in, d2_in, w2_in, k2_in,
    second, first, join,
    pressure, residual,
    far, s0, h0, ke0, kn0, d0, w0, k0, e0, g0, a0, b0,
    s1, h1, ke1, kn1, d1, w1, k1, e1, g1, a1, b1, s2, h2, ke2, kn2, d2, w2, k2, e2, g2, a2, b2, flat, nat, sems,
):
    def fill(high, low):
        for q in range(CELL):
            for g in range(2):
                lows = unfold([low[6 * q + 3 * g + i] for i in range(3)], 0)
                highs = unfold([high[6 * q + 3 * g + i] for i in range(3)], 0)
                for r, a, b in zip(range(4 * g, 4 * g + 4), highs, lows):
                    s_new = jnp.where(row_of(a) < 4, a, b)
                    h_new = pltpu.roll(jnp.where(row_of(a) < 4, b, a), 4, 0)
                    for to, inner, new in ((s0, s0_in, s_new), (h0, h0_in, h_new)):
                        to[q, r, 0:8, :] = inner[q, r, ROWS - 8 : ROWS, :]
                        to[q, r, 8:16, :] = new
                        to[q, r, 16:24, :] = inner[q, r, 0:8, :]
        for i in range(4):
            far[0, i] = high[6 * CELL + i]
            far[1, i] = low[6 * CELL + i]

    by_parity("lat", fill, first, second)

    levels = (
        (8, h0, ke0, kn0, s0, d0, w0, k0, e0, g0, a0, b0, (ke0_in, kn0_in, d0_in, w0_in, k0_in), it0_in),
        (4, h1, ke1, kn1, s1, d1, w1, k1, e1, g1, a1, b1, (ke1_in, kn1_in, d1_in, w1_in, k1_in), it1_in),
        (2, h2, ke2, kn2, s2, d2, w2, k2, e2, g2, a2, b2, (ke2_in, kn2_in, d2_in, w2_in, k2_in), it2_in),
    )
    source3 = []
    for i, (n, h, ke, kn, source, d, w, k, e, g, _, _, inner, _) in enumerate(levels):
        for r in range(n):
            h[n, r] = strip_of(north(Whole((h0_in, h1_in, h2_in)[i], h)[0, r]))
        find_faces(n, h, ke, kn)
        for r in range(n):
            kn[0, r] = strip_of(south(Whole(inner[1], kn)[n, r]))
        find_weights(n, ke, kn, source, d, w, k, e)
        sweep(n, ke, kn, w, k, e, g)
        if i < 2:
            s_next, s_inner, h_next = ((s1, s1_in, h1), (s2, s2_in, h2))[i]

            def put_s(q, r, x, s_next=s_next, s_inner=s_inner):
                s_next[q, r] = strip_of(merged(s_inner[q, r], x))

            def put_h(q, r, x, h_next=h_next):
                h_next[q, r] = x

            restrict(n, ke, kn, d, k, g, put_s)
            coarsen(n, h, put_h)
        else:
            restrict(n, ke, kn, d, k, g, lambda q, r, x: source3.append(x))

    strip = source3[0]
    s = merged(s3_in[0], strip)
    row = row_of(far[0, 0])
    s = jnp.concatenate(
        [
            s[0:ROWS],
            jnp.where(row < 2, strip[8:16], far[0, 0]),
            jnp.where(row < 4, far[0, 1], far[1, 1]),
            jnp.where(row >= 6, strip[8:16], far[1, 0]),
        ],
        axis=0,
    )
    h = jnp.concatenate([s3_in[1], far[0, 2], jnp.where(row < 4, far[0, 3], far[1, 3]), far[1, 2]], axis=0)
    ke, kn = jnp.minimum(h, east(h)), jnp.minimum(h, north(h))
    kw, ks = west(ke), south(kn)
    _, weight, s = weigh((ke + kw) + (kn + ks), s)
    v = weight * s
    for _ in range(COARSE_SWEEPS - 1):
        total = (ke * east(v) + kw * west(v)) + (kn * north(v) + ks * south(v))
        v = (1.0 - OMEGA) * v + weight * (s + total)
    coarse = jnp.concatenate([v[0:ROWS], jnp.where(row < 4, v[32:40], v[48:56])], axis=0)

    above = lambda q, r: coarse
    for n, _, ke, kn, _, d, w, k, _, g, a, b, inner, it in reversed(levels):
        for q in range(n):
            for r in range(n):
                a[q + 1, r] = merged(it[q + 1, r], g[q + 1, r]) + above(q // 2, r // 2)
        close(a, n)
        ke, kn, w, k = (Whole(x, y) for x, y in zip((inner[0], inner[1], inner[3], inner[4]), (ke, kn, w, k)))
        sweep(n, ke, kn, w, k, a, b)
        if n < CELL:
            sweep(n, ke, kn, w, k, b, a, final=True)
        above = lambda q, r, a=a: a[q + 1, r]

    def flatten(q, xs):
        lane = lane_of(xs[0])
        held = (lane >= LEAD) & (lane < LEAD + COLS)
        for r in range(4):
            x = jnp.where(held, xs[r], pltpu.roll(xs[r + 4], COLS, 1))
            flat[q * ROWS : (q + 1) * ROWS, r * LANES : (r + 1) * LANES] = x

    def finish(i, out):
        copies = []
        width = 2 * LANES
        for half in range(out.shape[1] // width):
            res = dot_parts(flat[...], join[:, half * width : (half + 1) * width], 2)
            for c in (2 * half, 2 * half + 1):
                at = slice((c - 2 * half) * LANES, (c - 2 * half + 1) * LANES)
                for q in range(CELL):
                    nat[i, c, pl.ds(q, ROWS, stride=CELL), :] = res[q * ROWS : (q + 1) * ROWS, at]
                copy = pltpu.make_async_copy(nat.at[i, c], out.at[:, c * LANES : (c + 1) * LANES], sems.at[i, c])
                copy.start()
                copies.append(copy)
        return copies

    sweep(8, ke, kn, w, k, b0, a0, flatten)
    copies = finish(0, pressure)
    inner = levels[0][12]
    ke, kn, d, k = (
        Whole(x, y, ROWS) for x, y in zip((inner[0], inner[1], inner[2], inner[4]), (ke0, kn0, d0, k0))
    )
    for q in range(CELL):
        flatten(q, remains(8, ke, kn, d, k, a0, q, ROWS))
    copies += finish(1, residual)
    for copy in copies:
        copy.wait()


def swap(x, axis, count, offset, closed):
    pairs = []
    for i in range(offset, count, 2):
        if i + 1 < count or closed:
            j = (i + 1) % count
            pairs += [(i, j), (j, i)]
    return lax.ppermute(x, axis, pairs)


def side_matrix(columns):
    out = np.zeros((2 * LANES, CELL * LANES), np.float32)
    c = np.arange(LANES - SIDE, LANES)
    out[c, (c % CELL) * LANES + LEAD + (c - LANES) // CELL] = 1.0
    c = np.arange(SIDE)
    out[LANES + c, (c % CELL) * LANES + LEAD + (columns + c) // CELL] = 1.0
    return jnp.asarray(out, jnp.bfloat16)


def join_matrix(columns):
    out = np.zeros((4 * LANES, columns), np.float32)
    c = np.arange(columns)
    r, lane = c % CELL, c // CELL + LEAD
    out[(r % 4) * LANES + np.where(r < 4, lane, (lane + COLS) % LANES), c] = 1.0
    return jnp.asarray(out, jnp.bfloat16)


VMEM = pl.BlockSpec(memory_space=pltpu.VMEM)
ANY = pl.BlockSpec(memory_space=pl.ANY)


def shaped(*dims):
    return jax.ShapeDtypeStruct(dims, jnp.float32)


def planes(n, more=0, rows=ROWS):
    return (n + more, n, rows, LANES)


def buffers(*shapes):
    return [pltpu.VMEM(s, jnp.float32) for s in shapes]


def limit(mib):
    return pltpu.CompilerParams(vmem_limit_bytes=mib * 1024 * 1024)


def cost(flops, moved):
    return pl.CostEstimate(flops=flops, bytes_accessed=moved, transcendentals=0)


def local(right_side, depth_level, ocean_mask):
    rows, columns = right_side.shape
    lon, lat = lax.axis_size("lon"), lax.axis_size("lat")
    side = pltpu.VMEM((2, rows, LANES), jnp.float32), pltpu.VMEM((2, rows, LANES), jnp.int32)
    first, second = pl.pallas_call(
        pack_kernel,
        out_shape=[shaped(2, 3 * rows // 4, LANES)] * 2,
        in_specs=[ANY] * 3,
        out_specs=[VMEM] * 2,
        scratch_shapes=[side[0], side[1], side[1], pltpu.SemaphoreType.DMA((2, 3))],
        compiler_params=limit(58),
    )(right_side, depth_level, ocean_mask)
    first = swap(first, "lon", lon, 0, True)
    second = swap(second, "lon", lon, 1, True)
    tiles = (columns // LANES, rows, LANES)
    own = pl.pallas_call(
        own_kernel,
        out_shape=[shaped(*planes(8))] * 2,
        in_specs=[VMEM] * 3,
        out_specs=[VMEM] * 2,
        scratch_shapes=buffers(tiles, tiles),
        compiler_params=limit(16),
        cost_estimate=cost(8 * rows * columns * CELL * LANES, 16 * rows * columns),
    )(right_side, depth_level, ocean_mask)

    message = shaped(6 * CELL + 4, 8, LANES)
    levels = (8, 4, 2)
    coefficients = [s for n in levels for s in (planes(n), planes(n, 1), planes(n), planes(n), planes(n))]
    fields = [s for n in levels for s in (planes(n), planes(n, 1))] + [(2, ROWS, LANES)] + [planes(n, 2) for n in levels]
    *fields, second, first = pl.pallas_call(
        down_kernel,
        out_shape=[shaped(*s) for s in fields + coefficients] + [message] * 2,
        in_specs=[VMEM] * 5,
        out_specs=[VMEM] * (len(fields) + len(coefficients) + 2),
        scratch_shapes=buffers(*[planes(n, 2) for n in levels]),
        compiler_params=limit(24),
    )(first, second, *own, side_matrix(columns))
    second = swap(second, "lat", lat, 1, False)
    first = swap(first, "lat", lat, 0, False)
    return pl.pallas_call(
        up_kernel,
        out_shape=[shaped(rows, columns)] * 2,
        in_specs=[VMEM] * (len(fields) + 3),
        out_specs=[ANY] * 2,
        scratch_shapes=buffers(
            (2, 4, 8, LANES),
            *[
                s
                for n in levels
                for s in (
                    planes(n, 0, 24), planes(n, 1, 24), planes(n, 0, 24), planes(n, 1, 24),
                    planes(n, 0, 24), planes(n, 0, 24), planes(n, 0, 24),
                    planes(n, 2, 24), planes(n, 2, 24), planes(n, 2, TALL), planes(n, 2, TALL),
                )
            ],
            (rows, 4 * LANES), (2, *tiles),
        ) + [pltpu.SemaphoreType.DMA((2, columns // LANES))],
        compiler_params=limit(24),
    )(*fields, second, first, join_matrix(columns))


def solution(mesh):
    placed = (P("lat", "lon"), P("lat", "lon"), P("lat", "lon"))
    return jax.shard_map(
        local,
        mesh=mesh,
        in_specs=placed,
        out_specs=(P("lat", "lon"), P("lat", "lon")),
        check_vma=False,
    )
```
